128 devices in a mesh: fsdp: 64 (over x_lo, y, z, core), rep: 2 (over x_hi).
Axes of the slice: x: 4 (x_hi: 2, x_lo: 2; x = x_hi * 2 + x_lo), y: 4, z: 4, core: 2. Of those that a mesh axis runs over, the one named last changes fastest.
Arguments:
- tokens: bfloat16 [16384, 1024], P(('fsdp', 'rep')), may hold values from -6 to 6
- segment_ids: int32 [256, 64], P(('fsdp', 'rep')), may hold values from 0 to 2, never falling along the last dimension, each value on 1 to 32 neighbouring positions
- routes: int32 [16384, 2], P(('fsdp', 'rep')), may hold values from 0 to 3, all different within a row; in each aligned block of 64 rows (0 to 63, 64 to 127, ...) at most 48 rows name the same one
- gain_attn: bfloat16 [1024], P('fsdp'), may hold values from 0.5 to 1.5
- attn_in: bfloat16 [1024, 2048], P('fsdp'), may hold values from -0.1875 to 0.1875
- attn_out: bfloat16 [1024, 1024], P('fsdp'), may hold values from -0.75 to 0.75
- gain_ffn: bfloat16 [1024], P('fsdp'), may hold values from 0.5 to 1.5
- router: bfloat16 [1024, 4], P('fsdp'), may hold values from -0.09375 to 0.09375
- expert_weight: bfloat16 [4096, 1536], P('fsdp'), may hold values from -0.375 to 0.375
- cotangent: bfloat16 [16384, 1024], P(('fsdp', 'rep')), may hold values from -6 to 6
Outputs:
- output: bfloat16 [16384, 1024], P(('fsdp', 'rep'))
- tokens_grad: float32 [16384, 1024], P(('fsdp', 'rep'))
- gain_attn_grad: float32 [1024], P('fsdp')
- attn_in_grad: float32 [1024, 2048], P('fsdp')
- attn_out_grad: float32 [1024, 1024], P('fsdp')
- gain_ffn_grad: float32 [1024], P('fsdp')
- router_grad: float32 [1024, 4], P('fsdp')
- expert_grad: float32 [4096, 1536], P('fsdp')
The draws below stay inside these ranges and needn't reach their ends.
Inputs may be any that keep to these rules, and one draw needn't show every extreme that they name: `segment_ids`: within each row the ids never fall and each sequence holds 1 to 32 tokens, one exactly 32. `routes`: each token names 2 different experts; within each aligned block of 64 rows (one micro-batch) no expert is named by more than 48 rows, and 48 is reached in some block.
All inputs are finite; a program needn't handle non-finite values.
Results may differ from the reference program's by a relative error of at most 0.015.
Values may be sent and summed in bfloat16 or wider, within the bound.
A program may use at most 192 MiB of HBM per device.

```python
import math
import jax
import jax.numpy as jnp
import numpy as np
from jax import lax

D = 1024
HEADS = 16
KV_HEADS = 8
HEAD_DIM = 64
FF = 512
EXPERTS = 4
TOP = 2
SEQS = 3
MB_TOK = 64
SEQ_MOST = 32
CAP = 48
TOKENS = 16384
BATCHES = 256


def steps_of(key, dims, split, least, top_value):
    loudness = 1.0
    for dim, shards_of in split:
        draws = jax.random.uniform(jax.random.fold_in(jax.random.fold_in(key, 6), dim), (shards_of,), jnp.float32, least / len(split), top_value / len(split))
        loudness = loudness * jnp.repeat(jnp.exp(draws), dims[dim] // shards_of).reshape((-1,) + (1,) * (len(dims) - 1 - dim))
    return loudness


def profile(amount, total, reach, lean):
    portions = [(1 << 20) // math.isqrt(grade ** lean) + 1 for grade in range(2, amount + 1)]
    spare, counts = total - reach - (amount - 1), [1] * (amount - 1)
    while spare > 0:
        candidates = [i for i in range(amount - 1) if counts[i] < reach]
        pool, remaining = sum([portions[i] for i in candidates]), spare
        for i in candidates:
            addition = min(reach - counts[i], max(1, remaining * portions[i] // pool), spare)
            counts[i] = counts[i] + addition
            spare = spare - addition
    return np.array([reach] + counts)


def ragged(key, count, total, bound, slope):
    if count == 2:
        one = jax.random.randint(key, (), max(1, total - bound), min(bound, total - 1) + 1)
        return jnp.stack([one, total - one])
    sizes = jnp.asarray(profile(count, total, bound, slope), jnp.int32)
    pairs = (count - 1) // 2
    donor, taker = sizes[1:1 + 2 * pairs:2], sizes[2:2 + 2 * pairs:2]
    margin = jnp.minimum(donor - 1, bound - taker)
    moved = jax.random.randint(jax.random.fold_in(key, 1), (pairs,), 0, 1 << 20) % (margin + 1)
    sizes = sizes.at[1:1 + 2 * pairs:2].set(donor - moved).at[2:2 + 2 * pairs:2].set(taker + moved)
    return sizes[jax.random.permutation(jax.random.fold_in(key, 2), count)]


def assign_block(own_key, own, number, rows, count, top, bound, skew):
    ranking = jax.random.permutation(own_key, count)
    heavy_load, usual = portions_of(count, rows * top, bound, skew, True), portions_of(count, rows * top, bound, skew, False)
    places = jnp.arange(count)

    def named(sizes, rotation):
        used = int((sizes > 0).sum())
        fixed = max(1, used // 4)
        passed = fixed + (places - fixed + rotation * (used - fixed)) % max(1, count - fixed)
        return jnp.zeros((count,), jnp.int32).at[ranking[jnp.where(places < fixed, places, passed)]].set(jnp.asarray(sizes, jnp.int32))

    sizes = jnp.where(number % 4 == 0, named(heavy_load, number // 4), named(usual, number - number // 4 - 1))
    mixed = jax.random.permutation(jax.random.fold_in(own, 3), count)
    donor, taker = mixed[0:count // 2 * 2:2], mixed[1:count // 2 * 2:2]
    room = jnp.minimum(sizes[donor] - 1, bound - sizes[taker]) // 2
    room = jnp.where((donor == ranking[0]) | (taker == ranking[0]) | (sizes[taker] == 0), 0, jnp.maximum(room, 0))
    passed = jax.random.randint(jax.random.fold_in(own, 4), (count // 2,), 0, 1 << 20) % (room + 1)
    sizes = sizes.at[donor].add(-passed).at[taker].add(passed)
    members = jnp.searchsorted(jnp.cumsum(sizes), jnp.arange(rows * top), side="right").astype(jnp.int32)
    listing = members.reshape(top, rows).T
    listing = listing[jax.random.permutation(jax.random.fold_in(own, 1), rows)]
    rotation = jax.random.randint(jax.random.fold_in(own, 2), (rows, 1), 0, top)
    return jnp.take_along_axis(listing, (jnp.arange(top)[None, :] + rotation) % top, axis=1)


def portions_of(count, total, reach, lean, full):
    loads = [(1 << 20) // math.isqrt(rank ** lean) + 1 for rank in range(1, count + 1)]
    largest = reach if full else min(reach, max(-(-total // count), total * loads[0] // sum(loads)))
    least = 1 if total - largest >= count - 1 else 0
    given, surplus = [largest] + [least] * (count - 1), total - largest - least * (count - 1)
    while surplus > 0:
        movable = [i for i in range(1, count) if given[i] < largest] or [i for i in range(1, count) if given[i] < reach]
        whole, left = sum([loads[i] for i in movable]), surplus
        for i in movable:
            more = min(reach - given[i], max(1, left * loads[i] // whole), surplus)
            given[i] = given[i] + more
            surplus = surplus - more
    return np.array(given)


def centred(key, dims, deviation, reach, shards=(), dtype=jnp.bfloat16):
    entries = deviation * jax.random.normal(key, dims, jnp.float32)
    if shards:
        entries = entries * steps_of(key, dims, shards, -0.22, 0.18)
    return jnp.clip(entries, -reach, reach).astype(dtype)


def setup_inputs(seed: int = 0) -> dict:
    streams_of = jax.random.split(jax.random.key(seed), 11)
    tokens = centred(streams_of[0], (TOKENS, D), 1.0, 6.0, ((0, 128),))
    segment_ids = jax.vmap(lambda own: jnp.searchsorted(jnp.cumsum(ragged(own, SEQS, MB_TOK, SEQ_MOST, 1)), jnp.arange(MB_TOK), side="right"))(jax.random.split(streams_of[1], BATCHES)).reshape((BATCHES, MB_TOK)).astype(jnp.int32)
    routes_keys = jax.random.split(jax.random.fold_in(streams_of[2], 1), TOKENS // MB_TOK)
    routes_turns = jax.random.permutation(jax.random.fold_in(streams_of[2], 3), TOKENS // MB_TOK)
    routes = jax.vmap(lambda own, number: assign_block(jax.random.fold_in(streams_of[2], 2), own, number, MB_TOK, EXPERTS, TOP, CAP, 2))(routes_keys, routes_turns).reshape((TOKENS, TOP))
    gain_attn = jnp.clip(1.0 + 0.1 * jax.random.normal(streams_of[3], (D,), jnp.float32), 0.5, 1.5).astype(jnp.bfloat16)
    attn_in = centred(streams_of[4], (D, HEADS * HEAD_DIM + 2 * KV_HEADS * HEAD_DIM), D ** -0.5, 0.1875, ((0, 64),))
    attn_out = centred(streams_of[5], (HEADS * HEAD_DIM, D), (HEADS * HEAD_DIM // 16) ** -0.5, 0.75, ((0, 64),))
    gain_ffn = jnp.clip(1.0 + 0.1 * jax.random.normal(streams_of[6], (D,), jnp.float32), 0.5, 1.5).astype(jnp.bfloat16)
    router = centred(streams_of[7], (D, EXPERTS), (4 * D) ** -0.5, 0.09375, ((0, 64),))
    expert_weight = centred(streams_of[8], (EXPERTS * D, 3 * FF), (D // 4) ** -0.5, 0.375, ((0, 64),))
    cotangent = centred(streams_of[9], (TOKENS, D), 1.0, 6.0, ((0, 128),))
    return {"tokens": tokens, "segment_ids": segment_ids, "routes": routes, "gain_attn": gain_attn, "attn_in": attn_in, "attn_out": attn_out, "gain_ffn": gain_ffn, "router": router, "expert_weight": expert_weight, "cotangent": cotangent}


EPS = 1e-06

@jax.custom_vjp
def low(v):
    return lax.optimization_barrier(v.astype(jnp.bfloat16)).astype(jnp.float32)

@jax.custom_vjp
def low_back(v):
    return v

def low_keep(v):
    return (low(v), None)

def low_pass(kept, grad):
    return (grad,)

def back_keep(v):
    return (v, None)

def back_low(kept, grad):
    return (low(grad),)
low.defvjp(low_keep, low_pass)
low_back.defvjp(back_keep, back_low)

def rope_tables(seg):
    count = seg.shape[0]
    index = jnp.arange(count)
    same = seg[:, None] == seg[None, :]
    before = index[None, :] < index[:, None]
    pos = lax.optimization_barrier(jnp.sum(jnp.where(same & before, 1.0, 0.0), axis=1))
    freq = 10000.0 ** (-(jnp.arange(HEAD_DIM // 2) * 2.0 / HEAD_DIM))
    angle = pos[:, None] * freq[None, :]
    allowed = same & (index[None, :] <= index[:, None])
    return (jnp.cos(angle), jnp.sin(angle), allowed)

def rotate(value, cosine, sine):
    half = HEAD_DIM // 2
    first = value[..., :half]
    second = value[..., half:]
    cos_b = cosine[:, None, :]
    sin_b = sine[:, None, :]
    return jnp.concatenate([first * cos_b - second * sin_b, second * cos_b + first * sin_b], axis=-1)

def slot_places(route):
    count = route.shape[0]
    onehot = (route[:, :, None] == jnp.arange(EXPERTS)[None, None, :]).astype(jnp.int32)
    flat = onehot.reshape(count * TOP, EXPERTS)
    earlier = jnp.cumsum(flat, axis=0) - flat
    slot = lax.optimization_barrier(jnp.sum(earlier * flat, axis=1)).reshape(count, TOP)
    return (route * CAP + slot).astype(jnp.int32)

def micro(x, seg, route, g1, win, wout, g2, wr, we):
    high = lax.Precision.HIGHEST
    count = x.shape[0]
    width_q = HEADS * HEAD_DIM
    width_k = KV_HEADS * HEAD_DIM
    group = HEADS // KV_HEADS
    r1 = lax.rsqrt(lax.optimization_barrier(jnp.mean(x * x, axis=1, keepdims=True)) + EPS)
    a1 = low(x * r1 * g1)
    qkv = low_back(jnp.dot(a1, win, precision=high))
    cosine, sine, allowed = rope_tables(seg)
    query = low(rotate(qkv[:, :width_q].reshape(count, HEADS, HEAD_DIM), cosine, sine))
    keys = low(rotate(qkv[:, width_q:width_q + width_k].reshape(count, KV_HEADS, HEAD_DIM), cosine, sine))
    values = low(qkv[:, width_q + width_k:].reshape(count, KV_HEADS, HEAD_DIM))
    grouped = query.reshape(count, KV_HEADS, group, HEAD_DIM)
    scores = low_back(jnp.einsum('tkgd,ukd->kgtu', grouped, keys, precision=high) * HEAD_DIM ** (-0.5))
    scores = jnp.where(allowed[None, None], scores, -1000000000.0)
    peak = lax.optimization_barrier(jnp.max(scores, axis=-1, keepdims=True))
    weights = jnp.exp(scores - peak)
    probs = weights / lax.optimization_barrier(jnp.sum(weights, axis=-1, keepdims=True))
    attn = jnp.einsum('kgtu,ukd->tkgd', low(probs), values, precision=high).reshape(count, width_q)
    attn = low(low_back(attn))
    hidden_state = x + low_back(jnp.dot(attn, wout, precision=high))
    r2 = lax.rsqrt(lax.optimization_barrier(jnp.mean(hidden_state * hidden_state, axis=1, keepdims=True)) + EPS)
    a2 = low(hidden_state * r2 * g2)
    logits = jnp.dot(a2, wr, precision=high)
    lpeak = lax.optimization_barrier(jnp.max(logits, axis=1, keepdims=True))
    lexp = jnp.exp(logits - lpeak)
    rprobs = lexp / lax.optimization_barrier(jnp.sum(lexp, axis=1, keepdims=True))
    gates = jnp.take_along_axis(rprobs, route, axis=1)
    place = slot_places(route).reshape(-1)
    expert_in = jnp.zeros((EXPERTS * CAP, x.shape[1]), jnp.float32).at[place].add(jnp.repeat(a2, TOP, axis=0))
    expert_in = expert_in.reshape(EXPERTS, CAP, x.shape[1])
    blocks = we.reshape(EXPERTS, x.shape[1], 3 * FF)
    gate_up = low_back(jnp.einsum('ecd,edf->ecf', expert_in, blocks[:, :, :2 * FF], precision=high))
    gate_part = gate_up[..., :FF]
    hidden = low(gate_part / (1.0 + jnp.exp(-gate_part)) * gate_up[..., FF:])
    expert_out = low_back(jnp.einsum('ecf,edf->ecd', hidden, blocks[:, :, 2 * FF:], precision=high))
    picked = expert_out.reshape(EXPERTS * CAP, x.shape[1])[place].reshape(count, TOP, x.shape[1])
    return hidden_state + lax.optimization_barrier(jnp.sum(gates[:, :, None] * picked, axis=1))

def reference(tokens, segment_ids, routes, gain_attn, attn_in, attn_out, gain_ffn, router, expert_weight, cotangent):
    width = tokens.shape[1]
    x_all = tokens.astype(jnp.float32).reshape(BATCHES, MB_TOK, width)
    route_all = routes.reshape(BATCHES, MB_TOK, TOP).astype(jnp.int32)

    def layer(x, g1, win, wout, g2, wr, we):

        def step(carry, item):
            xi, si, ri = item
            return (carry, micro(xi, si, ri, g1, win, wout, g2, wr, we))
        unused, outs = lax.scan(jax.checkpoint(step), jnp.zeros((), jnp.float32), (x, segment_ids, route_all))
        return outs
    params = (x_all, gain_attn.astype(jnp.float32), attn_in.astype(jnp.float32), attn_out.astype(jnp.float32), gain_ffn.astype(jnp.float32), router.astype(jnp.float32), expert_weight.astype(jnp.float32))
    result, pullback = jax.vjp(layer, *params)
    grads = pullback(cotangent.astype(jnp.float32).reshape(BATCHES, MB_TOK, width))
    return (result.reshape(-1, width).astype(jnp.bfloat16), grads[0].reshape(-1, width), grads[1], grads[2], grads[3], grads[4], grads[5], grads[6])
```

```python
import functools

import jax
import jax.numpy as jnp
from jax import lax
from jax.experimental import pallas as pl
from jax.experimental.pallas import tpu as pltpu
from jax.sharding import PartitionSpec as P

EPS = 1e-06
D = 1024
FF = 512
EXPERTS = 4
TOK = 128
COLS_W = 1536
SHARE = 768
ROWS_A = 16
ROWS_W = 64
MISC = 2048
EXTRA = 1152
HALF = 64
MESH = pl.DeviceIdType.MESH
F32 = jnp.float32
BF16 = jnp.bfloat16
WIDE = {"x": 2, "y": 4, "z": 4}

GATHERS = (
    (0, 0, 1024, "xyz"),
    (0, 1024, 1152, "xzy"),
    (1, 0, 512, "yzx"),
    (1, 512, 512, "zyx"),
    (2, 0, 384, "yz"),
    (2, 384, 384, "zy"),
)
SUMS = (
    (0, 0, 512, "xyz"),
    (0, 512, 512, "xzy"),
    (0, 1024, 512, "xyz"),
    (0, 1536, 512, "xzy"),
    (1, 0, 512, "yzx"),
    (1, 512, 640, "zyx"),
    (2, 0, 384, "yz"),
    (2, 384, 384, "zy"),
)
TILES = (0, 1, 4, 6, 2, 3, 5, 7)
INPUTS, OUTPUTS, EXPERTS_IN = (0, 1), (2, 3), (4, 5)
EARLY, LATE, OUT_SUMS, EXPERT_SUMS = (0, 1), (2, 3), (4, 5), (6, 7)
SUM_ORDER = EXPERT_SUMS + OUT_SUMS + EARLY + LATE
ROWS = (ROWS_A, ROWS_A, 2 * ROWS_W)


def unit_shape(unit):
    cores = (2,) if unit[0] < 2 else ()
    return cores + tuple(WIDE[axis] for axis in reversed(unit[3])) + (ROWS[unit[0]], unit[2])


def place():
    fsdp = lax.axis_index("fsdp")
    rep = lax.axis_index("rep")
    core = lax.rem(fsdp, 2)
    z = lax.rem(fsdp // 2, 4)
    y = lax.rem(fsdp // 8, 4)
    xl = fsdp // 32
    return {"x": xl, "y": y, "z": z, "c": core, "r": rep}


def device(at):
    return (at["x"] * 32 + at["y"] * 8 + at["z"] * 2 + at["c"], at["r"])


def shifted(at, axis, step):
    new = dict(at)
    if axis == "x":
        whole = lax.rem(at["r"] * 2 + at["x"] + step + 4, 4)
        new["x"] = lax.rem(whole, 2)
        new["r"] = whole // 2
    elif axis == "c":
        new["c"] = 1 - at["c"]
    else:
        new[axis] = lax.rem(at[axis] + step + 4, 4)
    return new


def greet(devices):
    barrier = pltpu.get_barrier_semaphore()
    for other in devices:
        pl.semaphore_signal(barrier, inc=1, device_id=device(other), device_id_type=MESH)


def meet(devices):
    pl.semaphore_wait(pltpu.get_barrier_semaphore(), len(devices))


ALL = slice(None)


class Piece:
    def __init__(self, order, spots, columns=ALL, rows=ALL):
        self.order, self.spots, self.columns, self.rows = order, spots, columns, rows

    def moved(self, axis, spot):
        return Piece(self.order, {**self.spots, axis: spot}, self.columns, self.rows)

    def full(self, axis):
        return self.moved(axis, (0, WIDE[axis]))

    def index(self, core, spots=None):
        spots = spots or self.spots
        lead = [spots[axis] for axis in reversed(self.order)]
        lead = [pl.ds(*spot) if isinstance(spot, tuple) else spot for spot in lead]
        return (*(() if core is None else (core,)), *lead, self.rows, self.columns)

    def of(self, ref, core):
        return ref.at[self.index(core)]

    def halves(self, rows, count):
        for axis in reversed(self.order):
            if isinstance(self.spots[axis], tuple):
                middle = WIDE[axis] // 2
                return [self.moved(axis, (0, middle)), self.moved(axis, (middle, middle))]
        first = count // 256 * 128
        return [Piece(self.order, self.spots, pl.ds(*run), ALL) for run in ((0, first), (first, count - first))]

    def shape(self, rows, count):
        lead = [self.spots[axis] for axis in reversed(self.order)]
        lead = tuple(spot[1] for spot in lead if isinstance(spot, tuple))
        size = [whole if part == ALL else part.size for part, whole in ((self.rows, rows), (self.columns, count))]
        return lead + tuple(size)


class Links:
    def __init__(self, at, send, recv, free, partners):
        self.at, self.send, self.recv, self.free, self.partners = at, send, recv, free, partners
        self.used, self.open = 0, []

    def turn(self):
        self.close()
        self.used, self.open = 0, []
        for other in self.partners:
            pl.semaphore_signal(self.free, inc=1, device_id=device(other), device_id_type=MESH)

    def turned(self):
        pl.semaphore_wait(self.free, len(self.partners))

    def local(self, source, target):
        copy = pltpu.make_async_copy(source, target, self.send.at[self.used])
        self.used += 1
        copy.start()
        return copy

    def push(self, source, target, to):
        copy = pltpu.make_async_remote_copy(
            src_ref=source,
            dst_ref=target,
            send_sem=self.send.at[self.used],
            recv_sem=self.recv.at[self.used],
            device_id=device(to),
            device_id_type=MESH,
        )
        self.used += 1
        copy.start()
        self.open.append(copy)
        return copy

    def close(self):
        for copy in self.open:
            copy.wait_send()


class Gather:
    def __init__(self, links, src, dst, unit):
        self.links, self.at, self.src, self.dst = links, links.at, src, dst
        array, self.first, self.count, self.order = unit
        self.rows = ROWS[array]
        self.core = self.at["c"] if array < 2 else None
        self.handed = []

    def push(self, source, piece, target):
        spot = piece.of(self.dst, self.core)
        return self.links.push(spot if source is None else source, spot, target)

    def sibling(self, piece, source=None):
        if self.core is None:
            return
        self.handed.append(self.push(source, piece, shifted(self.at, "c", 0)))

    def source_of(self, piece):
        columns = piece.columns
        if columns == ALL:
            columns = pl.ds(self.first, self.count)
        else:
            columns = pl.ds(self.first + columns.start, columns.size)
        return self.src.at[:, columns]

    def steps(self):
        at, order = self.at, self.order
        have = Piece(order, {axis: at[axis] for axis in order})
        if self.core is None:
            rows = pl.ds(pl.multiple_of(ROWS_W * at["c"], ROWS_W), ROWS_W)
            block = Piece(order, have.spots, ALL, rows)
            own, theirs = (src.at[:, pl.ds(self.first, self.count)] for src in self.src)
            local = self.links.local(own, block.of(self.dst, None))
            copy = self.push(theirs, block, shifted(at, "c", 0))
            yield
            local.wait()
            copy.wait_recv()
            mine = None
        else:
            mine = self.source_of(have)
            local = self.links.local(mine, have.of(self.dst, self.core))
        plane = order[:2] if order[0] == "x" else order[:1]
        ring = plane[-1]
        direct = [self.push(mine, have, shifted(at, ring, step)) for step in (1, -1, 2)]
        if "x" in plane:
            halves = have.halves(self.rows, self.count)
            for step in (0, 1, -1, 2):
                for half, side in zip(halves, (1, -1)):
                    target = shifted(shifted(at, "x", side), ring, step)
                    direct.append(self.push(self.source_of(half), half, target))
        yield
        if self.core is not None:
            local.wait()
        for copy in direct:
            copy.wait_recv()
        for axis in plane:
            have = have.full(axis)
        for axis in order[len(plane) :]:
            if axis == "x":
                halves = have.halves(self.rows, self.count)
                moved = [self.push(None, half, shifted(at, "x", side)) for half, side in zip(halves, (1, -1))]
                yield
                for copy in moved:
                    copy.wait_recv()
                self.sibling(have.moved("x", 1 - at["x"]))
                return
            near = [self.push(None, have, shifted(at, axis, step)) for step in (1, -1)]
            self.sibling(have)
            yield
            fresh = [have.moved(axis, shifted(at, axis, -step)[axis]) for step in (1, -1)]
            far = []
            for index, step in enumerate((1, -1)):
                near[index].wait_recv()
                piece = fresh[index].halves(self.rows, self.count)[index]
                far.append(self.push(None, piece, shifted(at, axis, step)))
            for piece in fresh:
                self.sibling(piece)
            yield
            for copy in far:
                copy.wait_recv()
            self.sibling(have.moved(axis, shifted(at, axis, 2)[axis]))
            have = have.full(axis)

    def settle(self):
        for copy in self.handed:
            copy.wait_recv()


class Group:
    def __init__(self, flows):
        self.flows = flows
        self.live = [flow.steps() for flow in flows]

    def step(self, times=1):
        for unused in range(times):
            self.live = [flow for flow in self.live if next(flow, "end") != "end"]

    def run(self):
        while self.live:
            self.step()

    def settle(self):
        self.run()
        for flow in self.flows:
            flow.settle()


def add_blocks(ref, piece, core, others):
    runs = [axis for axis in reversed(piece.order) if isinstance(piece.spots[axis], tuple)]
    loops = runs[:-1]
    total = 1
    for axis in loops:
        total *= piece.spots[axis][1]

    def step(i, carry):
        left, spots = i, dict(piece.spots)
        index = []
        for axis in reversed(loops):
            start, length = piece.spots[axis]
            spot = lax.rem(left, length)
            index.insert(0, spot)
            spots[axis] = start + spot
            left = left // length
        where = piece.index(core, spots)
        terms = [ref[where]]
        terms += [other[tuple(index) + (ALL,) * (len(other.shape) - len(index))] for other in others]
        if len(terms) > 2:
            terms = [term.astype(F32) for term in terms]
        ref[where] = functools.reduce(jnp.add, terms).astype(BF16)
        return carry

    if loops:
        lax.fori_loop(0, total, step, 0)
    else:
        step(0, 0)


class Scatter:
    def __init__(self, links, grad, out, unit, buffers):
        self.links, self.at, self.grad, self.out = links, links.at, grad, out
        array, self.first, self.count, self.order = unit
        self.unit, self.rows = unit, ROWS[array]
        self.buffers = list(buffers)

    @staticmethod
    def shapes(unit):
        rows, count, order = ROWS[unit[0]], unit[2], unit[3]
        piece = Piece(order, {axis: (0, WIDE[axis]) for axis in order})
        shapes = [piece.shape(rows, count)] if unit[0] < 2 else []
        rest = list(reversed(order))
        if order[-1] == "x":
            piece = piece.moved("x", 0)
            shapes += [half.shape(rows, count) for half in piece.halves(rows, count)]
            rest.pop(0)
        piece = piece.moved(rest[0], 0)
        shapes += [half.shape(rows, count) for half in piece.halves(rows, count)]
        shapes += [piece.shape(rows, count)] * 2
        shapes += [piece.moved(rest[1], 0).shape(rows, count)] * 3
        return shapes + [(rows, count)] * (3 if order[0] == "x" else 1)

    def push(self, piece, core, target):
        buffer = self.buffers.pop(0)
        return self.links.push(piece.of(self.grad, core), buffer, target), buffer

    def steps(self):
        at, rows, count = self.at, self.rows, self.count
        core = at["c"] if self.unit[0] < 2 else None
        piece = Piece(self.order, {axis: (0, WIDE[axis]) for axis in self.order})
        last = self.order[-1]
        if core is not None:
            copy, buffer = self.push(piece, 1 - core, shifted(at, "c", 0))
            yield
            copy.wait_recv()
            add_blocks(self.grad, piece, core, [buffer])
        rest = list(reversed(self.order))
        if last == "x":
            theirs = piece.moved("x", 1 - at["x"]).halves(rows, count)
            moved = [self.push(half, core, shifted(at, "x", step)) for half, step in zip(theirs, (1, -1))]
            yield
            piece = piece.moved("x", at["x"])
            for (copy, buffer), half in zip(moved, piece.halves(rows, count)):
                copy.wait_recv()
                add_blocks(self.grad, half, core, [buffer])
            rest.pop(0)
        last, ring = rest[:2]
        theirs = piece.moved(last, shifted(at, last, 2)[last]).halves(rows, count)
        far = [self.push(half, core, shifted(at, last, step)) for half, step in zip(theirs, (1, -1))]
        yield
        near = []
        for index, step in enumerate((1, -1)):
            theirs = piece.moved(last, shifted(at, last, step)[last])
            copy, buffer = far[index]
            copy.wait_recv()
            add_blocks(self.grad, theirs.halves(rows, count)[index], core, [buffer])
            near.append(self.push(theirs, core, shifted(at, last, step)))
        yield
        piece = piece.moved(last, at[last])
        for copy, buffer in near:
            copy.wait_recv()
        add_blocks(self.grad, piece, core, [buffer for copy, buffer in near])
        moves = [shifted(at, ring, step) for step in (1, -1, 2)]
        direct = [self.push(piece.moved(ring, to[ring]), core, to) for to in moves]
        yield
        piece = piece.moved(ring, at[ring])
        for copy, buffer in direct:
            copy.wait_recv()
        add_blocks(self.grad, piece, core, [buffer for copy, buffer in direct])
        if self.order[0] == "x":
            other = piece.moved("x", 1 - at["x"])
            piece = piece.moved("x", at["x"])
            ends = [self.push(piece, core, shifted(at, "x", 2))]
            ends += [self.push(other, core, shifted(at, "x", side)) for side in (1, -1)]
        else:
            ends = [self.push(piece, core, shifted(at, "x", 2))]
        yield
        for copy, buffer in ends:
            copy.wait_recv()
        total = self.grad[piece.index(core)].astype(F32) + ends[0][1][...].astype(F32)
        if len(ends) > 1:
            total = total + (ends[1][1][...].astype(F32) + ends[2][1][...].astype(F32))
        if core is not None:
            self.out[:, pl.ds(self.first, count)] = total
            return
        sums, shared, arriving = self.out
        lower = pl.multiple_of(ROWS_W * at["c"], ROWS_W)
        columns = pl.ds(self.first, count)
        shared[:, columns] = total
        theirs = shared.at[pl.ds(ROWS_W - lower, ROWS_W), columns]
        copy = self.links.push(theirs, arriving.at[:, columns], shifted(at, "c", 0))
        yield
        copy.wait_recv()
        for tile in range(self.first // 128, (self.first + count) // 128):
            local = pl.ds(128 * tile, 128)
            base = FF * (tile // 2) + 128 * (tile % 2)
            mine = pl.ds(pl.multiple_of(base + 256 * at["c"], 128), 128)
            other = pl.ds(pl.multiple_of(base + 256 * (1 - at["c"]), 128), 128)
            sums[:, mine] = shared[pl.ds(lower, ROWS_W), local]
            sums[:, other] = arriving[:, local]

    def settle(self):
        pass


def mm(a, b):
    return jnp.dot(a, b, preferred_element_type=F32)


def mm_nt(a, b):
    return lax.dot_general(a, b, (((1,), (1,)), ((), ())), preferred_element_type=F32)


def mm_tn(a, b):
    return lax.dot_general(a, b, (((0,), (0,)), ((), ())), preferred_element_type=F32)


def turn(value, cosine, sine):
    width = value.shape[1]
    lane = lax.broadcasted_iota(jnp.int32, (1, width), 1)
    low = lax.rem(lane, 64) < 32
    swapped = jnp.where(low, pltpu.roll(value, width - 32, 1), pltpu.roll(value, 32, 1))
    return value * cosine + swapped * sine


def doubled(block, odd, low):
    other = pltpu.roll(block.astype(F32), 64, 1).astype(BF16)
    return jnp.where(low, other, block) if odd else jnp.where(low, block, other)


def split_two(value):
    top = value.astype(BF16)
    return top, (value - top.astype(F32)).astype(BF16)


LAYER_SCRATCH = (
    pltpu.VMEM((ROWS_A, MISC + 128), BF16),
    pltpu.VMEM((ROWS_A, MISC), F32),
    pltpu.VMEM((ROWS_A, D + 128), F32),
    pltpu.VMEM((ROWS_W, SHARE), BF16),
    pltpu.VMEM((ROWS_W, SHARE), BF16),
    pltpu.VMEM((2 * ROWS_W, SHARE), F32),
    pltpu.VMEM((ROWS_W, SHARE), F32),
    pltpu.VMEM((TOK, 2048), BF16),
    pltpu.VMEM((TOK, D), BF16),
    pltpu.VMEM((8, 2 * TOK, TOK), F32),
    pltpu.VMEM((TOK, 2048), BF16),
    pltpu.VMEM((TOK, D), BF16),
    pltpu.VMEM((TOK, D), BF16),
    pltpu.VMEM((TOK, D), F32),
    pltpu.VMEM((TOK, D), F32),
    pltpu.VMEM((TOK, D), F32),
    pltpu.VMEM((D, TOK), BF16),
    pltpu.VMEM((D, TOK), BF16),
    pltpu.VMEM((4 * TOK, EXTRA), BF16),
    pltpu.VMEM((4 * TOK, D), BF16),
    pltpu.VMEM((2, 4 * TOK, SHARE), BF16),
    pltpu.VMEM((2 * TOK, D), F32),
    pltpu.VMEM((2 * TOK, D), F32),
    pltpu.VMEM((4 * TOK, 128), F32),
    pltpu.VMEM((2 * TOK, EXTRA), BF16),
    pltpu.VMEM((2 * TOK, EXTRA), BF16),
    pltpu.VMEM((TOK, EXTRA), BF16),
    pltpu.VMEM((TOK, EXTRA), BF16),
    pltpu.VMEM((2 * TOK, D), BF16),
    pltpu.VMEM((2 * TOK, D), BF16),
    pltpu.VMEM((TOK, D), BF16),
    pltpu.VMEM((TOK, D), BF16),
    pltpu.VMEM((D, 4 * TOK), BF16),
    pltpu.VMEM((D, 4 * TOK), BF16),
)


def whole_body(
    x_ref, g_ref, seg_ref, route_ref, in_ref, aout_ref, gain1_ref, gain2_ref, router_ref, expert_ref,
    out_ref, dx_ref, sum_in, sum_out, small_ref, sum_w,
    src_in, sum_all, sum_more, src_own, src_peer, shared, arriving, qkv, attn, probs, dqkv, a1_ref, dattn_ref, h_ref, dh_ref, da1_ref, a1t, attnt,
    a2_all, g_all, mid, da2_ref, y_ref, dg_ref, sib_d, from_d, ret_d, got_d, sib_y, from_y, ret_y, got_y, a2t, gt, *rest,
):
    at = place()
    ahead, behind = shifted(at, "x", 1), shifted(at, "x", -1)

    around = [shifted(at, axis, step) for axis in "yz" for step in (1, -1, 2)]
    around += [shifted(shifted(at, "x", side), axis, step) for axis in "yz" for step in (1, -1, 2) for side in (1, -1)]
    around += [shifted(at, "x", step) for step in (1, -1, 2)]
    around += [shifted(at, "c", 0)]
    links = Links(at, *rest[-5:-2], around)
    pairs = Links(at, *rest[-2:], None, None)
    greet(around)

    eight = lax.broadcasted_iota(jnp.int32, (8, 128), 0)
    eye = jnp.where(eight == lax.broadcasted_iota(jnp.int32, (8, 128), 1), 1.0, 0.0)
    small = [ref[...].astype(F32) for ref in (router_ref, gain1_ref, gain2_ref)]
    small = jnp.concatenate(small + [jnp.zeros((2, ROWS_A), F32)], axis=0)
    src_in[:, pl.ds(MISC, 128)] = mm_tn(small.astype(BF16), eye.astype(BF16)).astype(BF16)
    for slot, tile in enumerate(TILES):
        src_in[:, pl.ds(256 * slot, 256)] = in_ref[:, pl.ds(256 * tile, 256)]

    for index in range(3):
        target = pl.ds(256 * index, 256)
        for half, columns in ((at["c"], src_own), (1 - at["c"], src_peer)):
            columns[:, target] = expert_ref[:, pl.ds(pl.multiple_of(FF * index + 256 * half, 256), 256)]

    meet(around)

    sources = (src_in, aout_ref, (src_own, src_peer))
    sums = (sum_all, sum_more, (sum_w, shared, arriving))
    buffers = list(rest[:-5])

    weights, grads = buffers[: len(GATHERS)], buffers[len(GATHERS) : len(GATHERS) + len(SUMS)]
    del buffers[: len(GATHERS) + len(SUMS)]

    def gathers(units):
        return Group([Gather(links, sources[GATHERS[u][0]], weights[u], GATHERS[u]) for u in units])

    def scatters(*units):
        flows = []
        for u in units:
            number = len(Scatter.shapes(SUMS[u]))
            mine = buffers[:number]
            del buffers[:number]
            flows.append(Scatter(links, grads[u], sums[SUMS[u][0]], SUMS[u], mine))
        return Group(flows)

    def swap(source, target, first_source, first_target):
        rows = ((0, ahead), (HALF, behind))
        return [
            pairs.push(
                source.at[pl.ds(first_source + lower, HALF)], target.at[pl.ds(first_target + lower, HALF)], to
            )
            for lower, to in rows
        ]

    def swap_back(source, target):
        rows = ((0, behind), (HALF, ahead))
        return [
            pairs.push(source.at[pl.ds(lower, HALF)], target.at[pl.ds(lower, HALF)], to) for lower, to in rows
        ]

    def arrived(copies):
        for copy in copies:
            copy.wait_recv()

    def spot(unit, **where):
        return tuple(where[axis] for axis in ("c",) + tuple(reversed(unit[3])))

    def blocks_a(xs=(0, 1), ys=(0, 1, 2, 3)):
        return [dict(x=x, y=y, z=z, c=c) for x in xs for y in ys for z in range(4) for c in range(2)]

    def cols_a(u, lower, count, **some):
        return jnp.concatenate(
            [weights[u][spot(GATHERS[u], **where) + (ALL, pl.ds(lower, count))] for where in blocks_a(**some)],
            axis=0,
        )

    def tile_a(u, t, count, lower=0):
        return cols_a(u, lower, count, xs=(t // 2,), ys=(2 * (t % 2), 2 * (t % 2) + 1))

    def put_a(u, lower, value):
        value, count = value.astype(BF16), value.shape[1]
        for i, where in enumerate(blocks_a()):
            grads[u][spot(SUMS[u], **where) + (ALL, pl.ds(lower, count))] = value[ROWS_A * i : ROWS_A * (i + 1)]

    def blocks_w(el, ys=(0, 1), zs=(0, 1, 2, 3)):
        return [dict(y=2 * el + y, z=z) for y in ys for z in zs]

    def spot_w(unit, y, z):
        return (z, y) if unit[3] == "yz" else (y, z)

    def cols_w(el, lower, count, **some):
        runs = []
        for u, start in zip(EXPERTS_IN, (0, 384)):
            low_col, high_col = max(lower, start), min(lower + count, start + 384)
            if low_col < high_col:
                columns = pl.ds(low_col - start, high_col - low_col)
                blocks = [weights[u][spot_w(GATHERS[u], **at_w) + (ALL, columns)] for at_w in blocks_w(el, **some)]
                runs.append(jnp.concatenate(blocks, axis=0))
        return runs[0] if len(runs) == 1 else jnp.concatenate(runs, axis=1)

    def put_w(el, lower, value):
        value, count = value.astype(BF16), value.shape[1]
        for u, start in zip(EXPERT_SUMS, (0, 384)):
            low_col, high_col = max(lower, start), min(lower + count, start + 384)
            if low_col < high_col:
                columns = pl.ds(low_col - start, high_col - low_col)
                for i, at_w in enumerate(blocks_w(el)):
                    block = value[128 * i : 128 * (i + 1), low_col - lower : high_col - lower]
                    grads[u][spot_w(SUMS[u], **at_w) + (ALL, columns)] = block

    inputs, outputs, experts = gathers(INPUTS), gathers(OUTPUTS), gathers(EXPERTS_IN)
    inputs.step()
    experts.step()

    own = pl.ds(0, TOK)
    g_all[own, :] = g_ref[...]
    x = x_ref[...].astype(F32)
    r1 = lax.rsqrt(jnp.mean(x * x, axis=1, keepdims=True) + EPS)
    ids = jnp.concatenate([seg_ref[0:1, :], seg_ref[1:2, :] + 4], axis=1).astype(F32)
    rows = jnp.concatenate([ids, route_ref[...].astype(F32), jnp.zeros((TOK - 3, TOK), F32)], axis=0)
    columns = rows.T
    lane = lax.broadcasted_iota(jnp.int32, (1, 128), 1)
    low = lane < 64
    same = columns[:, 0:1] == ids
    t_index = lax.broadcasted_iota(jnp.int32, (TOK, TOK), 0)
    u_index = lax.broadcasted_iota(jnp.int32, (TOK, TOK), 1)
    pos = jnp.sum(jnp.where(same & (u_index < t_index), 1.0, 0.0), axis=1, keepdims=True)
    allowed = same & (u_index <= t_index)
    allowed2 = jnp.concatenate([allowed, allowed], axis=0)
    route0, route1 = columns[:, 1:2].astype(jnp.int32), columns[:, 2:3].astype(jnp.int32)
    named = (route0 == lane) | (route1 == lane)
    inputs.step()
    outputs.step()
    power = lax.rem(lane, 32).astype(F32) * (2.0 / 64)
    angle = pos * jnp.exp(power * (-9.210340371976184))
    cosine = jnp.cos(angle)
    sine = jnp.where(lax.rem(lane, 64) < 32, -1.0, 1.0) * jnp.sin(angle)
    cos4 = jnp.concatenate([cosine] * 2, axis=1)
    sin4 = jnp.concatenate([sine] * 2, axis=1)
    inputs.step()
    outputs.step()
    experts.step()
    inputs.run()
    outputs.step()
    experts.step()
    inputs.settle()

    misc = cols_a(1, 1024, 128)
    row = lax.broadcasted_iota(jnp.int32, (16, 128), 0)
    lane16 = lax.broadcasted_iota(jnp.int32, (16, 128), 1)
    gains = mm_nt(jnp.where(lane16 == row + 4, 1.0, 0.0).astype(BF16), misc)
    gain1, gain2 = gains[0:1], gains[1:2]
    a1_ref[...] = (x * r1 * gain1).astype(BF16)
    for j in range(8):
        block = mm(a1_ref[...], cols_a(j // 4, 256 * (j % 4), 256))
        if TILES[j] < 6:
            block = turn(block, cos4, sin4)
        qkv[:, pl.ds(256 * TILES[j], 256)] = block.astype(BF16)
        if j == 0:
            g_copies = swap(g_ref, g_all, 0, TOK)
            g_own = pairs.push(g_ref, g_all.at[pl.ds(2 * TOK, TOK)], shifted(at, "c", 0))
    outputs.step()

    def heads(ref, k):
        pair = ref[:, pl.ds(128 * k, 128)]
        zero = jnp.zeros_like(pair)
        return jnp.concatenate([jnp.where(low, pair, zero), jnp.where(low, zero, pair)], axis=0)

    def keys(k):
        return doubled(qkv[:, pl.ds(1024 + 128 * (k // 2), 128)], k % 2, low)

    def values(k):
        return doubled(qkv[:, pl.ds(1536 + 128 * (k // 2), 128)], k % 2, low)

    for first in (0, 4):
        some = range(first, first + 4)
        scores = [mm_nt(heads(qkv, k), keys(k)) * 0.125 for k in some]
        scores = [jnp.where(allowed2, score, -1000000000.0) for score in scores]
        peaks = [jnp.max(score, axis=1, keepdims=True) for score in scores]
        raised = [jnp.exp(score - peak) for score, peak in zip(scores, peaks)]
        scales = [1.0 / jnp.sum(value, axis=1, keepdims=True) for value in raised]
        prob = [value * scale for value, scale in zip(raised, scales)]
        both = [mm(value.astype(BF16), values(k)) for value, k in zip(prob, some)]
        for k, value, pair in zip(some, prob, both):
            probs[k] = value
            attn[:, pl.ds(128 * k, 128)] = jnp.where(low, pair[:TOK], pair[TOK:]).astype(BF16)
        if first == 0:
            outputs.run()
        else:
            experts.step()
    a1t[...] = a1_ref[...].T
    outputs.settle()

    for j in range(4):
        part_j = pl.ds(256 * j, 256)
        h_ref[:, part_j] = x_ref[:, part_j].astype(F32) + mm(
            attn[...], cols_a(OUTPUTS[j // 2], 256 * (j % 2), 256)
        )
    h = h_ref[...]
    r2 = lax.rsqrt(jnp.mean(h * h, axis=1, keepdims=True) + EPS)
    a2 = (h * r2 * gain2).astype(BF16)
    a2_all[own, pl.ds(0, D)] = a2
    logits = jnp.where(lane < EXPERTS, mm(a2, misc), -jnp.inf)
    lexp = jnp.exp(logits - jnp.max(logits, axis=1, keepdims=True))
    rprobs = lexp / jnp.sum(lexp, axis=1, keepdims=True)
    gates = jnp.where(named, rprobs, 0.0)
    top, rest_of = split_two(gates)
    a2_all[own, pl.ds(D, 128)] = (top.astype(F32) + pltpu.roll(rest_of.astype(F32), EXPERTS, 1)).astype(BF16)
    a2_copies = swap(a2_all, a2_all, 0, TOK)
    experts.run()
    sibling = shifted(at, "c", 0)
    beside, across = pl.ds(TOK, TOK), pl.ds(3 * TOK, TOK)
    a2_own = pairs.push(a2_all.at[own], a2_all.at[pl.ds(2 * TOK, TOK)], sibling)
    arrived(g_copies)
    g_on = pairs.push(g_all.at[beside], g_all.at[across], sibling)
    arrived([g_own, g_on])
    gt[...] = g_all[...].T
    attnt[...] = attn[...].T
    experts.settle()
    links.turn()
    arrived(a2_copies)
    a2_on = pairs.push(a2_all.at[beside], a2_all.at[across], sibling)
    arrived([a2_own, a2_on])

    dgates = jnp.zeros((4 * TOK, 128), F32)
    for el in range(2):
        e = 2 * at["x"] + el
        extra = a2_all[:, pl.ds(D, 128)].astype(F32)
        gate_e = jnp.sum(jnp.where((lane == e) | (lane == e + EXPERTS), extra, 0.0), axis=1, keepdims=True)
        v = mm(a2_all[:, pl.ds(0, D)], cols_w(el, 0, 256))
        up = mm(a2_all[:, pl.ds(0, D)], cols_w(el, 256, 256))
        back = mm(g_all[...], cols_w(el, 512, 256))
        s = 1.0 / (1.0 + jnp.exp(-v))
        silu = v * s
        hidden = (silu * up).astype(BF16).astype(F32)
        dgates = dgates + jnp.where(lane == e, jnp.sum(hidden * back, axis=1, keepdims=True), 0.0)
        back = back * gate_e
        mid[el, :, pl.ds(0, 256)] = (back * up * s * (1.0 + v * (1.0 - s))).astype(BF16)
        mid[el, :, pl.ds(256, 256)] = (back * silu).astype(BF16)
        mid[el, :, pl.ds(512, 256)] = (hidden * gate_e).astype(BF16)
    dg_ref[...] = dgates

    def tile_w(el, t, lower, count):
        return cols_w(el, lower, count, ys=(t // 2,), zs=(2 * lax.rem(t, 2), 2 * lax.rem(t, 2) + 1))

    def da2_tile(t, carry):
        total = jnp.zeros((4 * TOK, 256), F32)
        for el in range(2):
            total = total + mm_nt(mid[el, :, pl.ds(0, 512)], tile_w(el, t, 0, 512))
        columns = pl.ds(pl.multiple_of(256 * t, 256), 256)
        da2_ref[:, columns] = total[: 2 * TOK]
        sib_d[:, columns] = total[2 * TOK :].astype(BF16)
        return carry

    def two_lanes(value):
        top, rest_of = split_two(value)
        return (top.astype(F32) + pltpu.roll(rest_of.astype(F32), EXPERTS, 1)).astype(BF16)

    def one_lane(extra):
        extra = extra.astype(F32)
        return extra + pltpu.roll(extra, 128 - EXPERTS, 1)

    lax.fori_loop(0, 4, da2_tile, 0)
    gates_at = pl.ds(D, 128)
    sib_d[:, gates_at] = two_lanes(dg_ref[pl.ds(2 * TOK, 2 * TOK), :])
    sib_copy = pairs.push(sib_d, from_d, sibling)
    a2t[...] = a2_all[:, pl.ds(0, D)].T
    sib_copy.wait_recv()
    ret_d[:, pl.ds(0, D)] = (da2_ref[beside, :] + from_d[beside, pl.ds(0, D)].astype(F32)).astype(BF16)
    ret_d[:, gates_at] = two_lanes(
        jnp.where(lane < EXPERTS, dg_ref[beside, :] + one_lane(from_d[beside, gates_at]), 0.0)
    )
    d_copies = swap_back(ret_d, got_d)

    for el in range(2):
        for j in range(3):
            left = a2t if j < 2 else gt
            put_w(el, 256 * j, mm(left[...], mid[el, :, pl.ds(256 * j, 256)]))
    links.turned()
    expert_sums = scatters(*EXPERT_SUMS)
    expert_sums.step()

    def y_tile(t, carry):
        total = jnp.zeros((4 * TOK, 256), F32)
        for el in range(2):
            total = total + mm_nt(mid[el, :, pl.ds(512, 256)], tile_w(el, t, 512, 256))
        columns = pl.ds(pl.multiple_of(256 * t, 256), 256)
        y_ref[:, columns] = total[: 2 * TOK]
        sib_y[:, columns] = total[2 * TOK :].astype(BF16)
        return carry

    lax.fori_loop(0, 4, y_tile, 0)
    y_own = pairs.push(sib_y, from_y, sibling)

    arrived(d_copies)
    dgates = dg_ref[own, :] + one_lane(from_d[own, gates_at]) + one_lane(got_d[:, gates_at])
    dp = jnp.where(named, dgates, 0.0)
    dlogits = (rprobs * (dp - jnp.sum(rprobs * dp, axis=1, keepdims=True))).astype(BF16)
    da2 = da2_ref[own, :] + from_d[own, pl.ds(0, D)].astype(F32) + got_d[:, pl.ds(0, D)].astype(F32)
    da2 = da2 + mm_nt(dlogits, misc)
    h = h_ref[...]
    misc_grad = mm_tn(a2_all[own, pl.ds(0, D)], dlogits)
    gain_two = (da2 * h * r2).astype(BF16)
    scaled = gain2 * da2
    dh = g_ref[...].astype(F32) + r2 * scaled - h * (r2 * r2 * r2) * jnp.mean(scaled * h, axis=1, keepdims=True)
    branch = dh.astype(BF16)
    dh_ref[...] = dh
    for j in range(4):
        put_a(OUT_SUMS[j // 2], 256 * (j % 2), mm(attnt[...], branch[:, 256 * j : 256 * j + 256]))
    misc_grad = misc_grad + mm_tn(gain_two, jnp.where(u_index == 5, 1.0, 0.0).astype(BF16))
    put_a(OUT_SUMS[1], 512, misc_grad)
    out_sums = scatters(*OUT_SUMS)
    out_sums.step()
    for t in range(4):
        dattn = mm_nt(branch[:, :512], tile_a(OUTPUTS[0], t, 512)) + mm_nt(branch[:, 512:], tile_a(OUTPUTS[1], t, 512))
        dattn_ref[:, pl.ds(256 * t, 256)] = dattn.astype(BF16)

    y_own.wait_recv()
    ret_y[...] = (y_ref[beside, :] + from_y[beside, :].astype(F32)).astype(BF16)
    y_copies = swap_back(ret_y, got_y)
    for first in (0, 4):
        some = range(first, first + 4)
        stacks = [heads(dattn_ref, k) for k in some]
        dprob = [mm_nt(stack, values(k)) for stack, k in zip(stacks, some)]
        parts = [probs[k] * value for k, value in zip(some, dprob)]
        sums_of = [jnp.sum(value, axis=1, keepdims=True) for value in parts]
        ds = [(value - probs[k] * total).astype(BF16) for k, value, total in zip(some, parts, sums_of)]
        dq = [mm(value, keys(k)) * 0.125 for value, k in zip(ds, some)]
        dk = [mm_tn(value, heads(qkv, k)) * 0.125 for value, k in zip(ds, some)]
        dv = [mm_tn(probs[k].astype(BF16), stack) for k, stack in zip(some, stacks)]
        dk = [value + pltpu.roll(value, 64, 1) for value in dk]
        dv = [value + pltpu.roll(value, 64, 1) for value in dv]
        for k, value in zip(some, dq):
            value = jnp.where(low, value[:TOK], value[TOK:])
            dqkv[:, pl.ds(128 * k, 128)] = turn(value, cosine, -sine).astype(BF16)
        for i in (0, 2):
            column = 64 * (first + i)
            value = turn(jnp.where(low, dk[i], dk[i + 1]), cosine, -sine)
            dqkv[:, pl.ds(1024 + column, 128)] = value.astype(BF16)
            dqkv[:, pl.ds(1536 + column, 128)] = jnp.where(low, dv[i], dv[i + 1]).astype(BF16)
        if first == 0:
            early = scatters(*EARLY)
            for j in range(4):
                put_a(j // 2, 256 * (j % 2), mm(a1t[...], dqkv[:, pl.ds(256 * TILES[j], 256)]))
            early.step()
            expert_sums.step()
            out_sums.step()
    late = [scatters(u) for u in LATE]
    for j in range(4, 8):
        put_a(j // 2, 256 * (j % 2), mm(a1t[...], dqkv[:, pl.ds(256 * TILES[j], 256)]))
        if j % 2:
            late[j // 2 - 2].step()
    early.step()
    out_sums.step()
    expert_sums.step()
    for t in range(4):
        total = jnp.zeros((TOK, 256), F32)
        for j in range(8):
            left = dqkv[:, pl.ds(256 * TILES[j], 256)]
            total = total + mm_nt(left, tile_a(j // 4, t, 256, 256 * (j % 4)))
        da1_ref[:, pl.ds(256 * t, 256)] = total
    da1 = da1_ref[...]
    x = x_ref[...].astype(F32)
    for group in late:
        group.step()
    scaled = gain1 * da1
    dx_ref[...] = (
        dh_ref[...] + r1 * scaled - x * (r1 * r1 * r1) * jnp.mean(scaled * x, axis=1, keepdims=True)
    )
    for group in late:
        group.step()
    early.step()
    out_sums.step()
    arrived(y_copies)
    out_ref[...] = (
        h_ref[...] + y_ref[own, :] + from_y[own, :].astype(F32) + got_y[...].astype(F32)
    ).astype(BF16)
    groups = late + [early, out_sums, expert_sums]
    while any(group.live for group in groups):
        for group in groups:
            group.step()
    product = jnp.zeros((ROWS_A, 1), F32)
    for slot, tile in enumerate(TILES):
        block = sum_all[:, pl.ds(256 * slot, 256)]
        sum_in[:, pl.ds(256 * tile, 256)] = block
        product = product + jnp.sum(block * in_ref[:, pl.ds(256 * tile, 256)].astype(F32), axis=1, keepdims=True)
    sum_out[...] = sum_more[:, pl.ds(0, D)]
    own_gain = jnp.sum(jnp.where(lane == 4, src_in[:, pl.ds(MISC, 128)].astype(F32), 0.0), axis=1, keepdims=True)
    tail = jnp.where(lane == 4, product / own_gain, sum_more[:, pl.ds(D, 128)])
    tail = jnp.concatenate([tail, jnp.zeros((128 - ROWS_A, 128), F32)], axis=0)
    small_ref[...] = tail.T[:8, :ROWS_A]
    links.close()
    pairs.close()


SEMS = 90
PAIR_SEMS = 14
VMEM_LIMIT = 60 * 1024 * 1024


def whole(tokens, cotangent, seg, routes, attn_in, attn_out, gain_attn, gain_ffn, router, expert_weight):
    buffers = [pltpu.VMEM(unit_shape(unit), BF16) for unit in GATHERS + SUMS]
    buffers += [pltpu.VMEM(shape, BF16) for u in SUM_ORDER for shape in Scatter.shapes(SUMS[u])]
    vmem = pl.BlockSpec(memory_space=pltpu.VMEM)
    return pl.pallas_call(
        whole_body,
        out_shape=(
            jax.ShapeDtypeStruct((TOK, D), BF16),
            jax.ShapeDtypeStruct((TOK, D), F32),
            jax.ShapeDtypeStruct((ROWS_A, 2048), F32),
            jax.ShapeDtypeStruct((ROWS_A, D), F32),
            jax.ShapeDtypeStruct((8, ROWS_A), F32),
            jax.ShapeDtypeStruct((ROWS_W, COLS_W), F32),
        ),
        in_specs=[vmem] * 10,
        out_specs=(vmem,) * 6,
        scratch_shapes=list(LAYER_SCRATCH)
        + buffers
        + [pltpu.SemaphoreType.DMA((SEMS,)), pltpu.SemaphoreType.DMA((SEMS,)), pltpu.SemaphoreType.REGULAR]
        + [pltpu.SemaphoreType.DMA((PAIR_SEMS,))] * 2,
        compiler_params=pltpu.CompilerParams(
            collective_id=0, has_side_effects=True, vmem_limit_bytes=VMEM_LIMIT
        ),
    )(tokens, cotangent, seg, routes, attn_in, attn_out, gain_attn, gain_ffn, router, expert_weight)


def emit_body(*refs):
    big, small, outs = refs[:5], refs[5], refs[6:]
    for source, target in zip(big, outs):
        target[...] = source[...]
    router, gain1, gain2 = outs[5:]
    router[...] = small[0:4, :]
    gain1[...] = small[4:5, :]
    gain2[...] = small[5:6, :]


def emit(big, small):
    vmem = pl.BlockSpec(memory_space=pltpu.VMEM)
    shapes = [jax.ShapeDtypeStruct(value.shape, value.dtype) for value in big]
    shapes += [jax.ShapeDtypeStruct((rows, ROWS_A), F32) for rows in (EXPERTS, 1, 1)]
    return pl.pallas_call(
        emit_body, out_shape=tuple(shapes), in_specs=[vmem] * 6, out_specs=(vmem,) * 8
    )(*big, small)


def local(
    tokens, segment_ids, routes, gain_attn, attn_in, attn_out, gain_ffn, router, expert_weight, cotangent
):
    output, grad, sum_in, sum_out, small, sum_w = whole(
        tokens, cotangent, segment_ids, routes.T, attn_in, attn_out,
        gain_attn[None, :], gain_ffn[None, :], router.T, expert_weight,
    )
    output, grad, sum_in, sum_out, sum_w, router_grad, gain1, gain2 = emit(
        (output, grad, sum_in, sum_out, sum_w), small
    )
    return (output, grad, gain1[0], sum_in, sum_out, gain2[0], router_grad.T, sum_w)


def solution(mesh):
    return jax.shard_map(
        local,
        mesh=mesh,
        in_specs=(
            P(("fsdp", "rep"), None),
            P(("fsdp", "rep"), None),
            P(("fsdp", "rep"), None),
            P("fsdp"),
            P("fsdp", None),
            P("fsdp", None),
            P("fsdp"),
            P("fsdp", None),
            P("fsdp", None),
            P(("fsdp", "rep"), None),
        ),
        out_specs=(
            P(("fsdp", "rep"), None),
            P(("fsdp", "rep"), None),
            P("fsdp"),
            P("fsdp", None),
            P("fsdp", None),
            P("fsdp"),
            P("fsdp", None),
            P("fsdp", None),
        ),
        check_vma=False,
    )
```

```python
import functools

import jax
import jax.numpy as jnp
from jax import lax
from jax.experimental import pallas as pl
from jax.experimental.pallas import tpu as pltpu
from jax.sharding import PartitionSpec as P

EPS = 1e-06
D = 1024
FF = 512
EXPERTS = 4
TOK = 128
COLS_W = 1536
SHARE = 768
ROWS_A = 16
ROWS_W = 64
MISC = 2048
EXTRA = 1152
HALF = 64
MESH = pl.DeviceIdType.MESH
F32 = jnp.float32
BF16 = jnp.bfloat16
WIDE = {"x": 2, "y": 4, "z": 4}

GATHERS = (
    (0, 0, 1024, "xyz"),
    (0, 1024, 1152, "xzy"),
    (1, 0, 512, "yzx"),
    (1, 512, 512, "zyx"),
    (2, 0, 384, "yz"),
    (2, 384, 384, "zy"),
)
SUMS = (
    (0, 0, 512, "xyz"),
    (0, 512, 512, "xzy"),
    (0, 1024, 512, "xyz"),
    (0, 1536, 512, "xzy"),
    (1, 0, 512, "yzx"),
    (1, 512, 640, "zyx"),
    (2, 0, 384, "yz"),
    (2, 384, 384, "zy"),
)
TILES = (0, 1, 4, 6, 2, 3, 5, 7)
INPUTS, OUTPUTS, EXPERTS_IN = (0, 1), (2, 3), (4, 5)
EARLY, LATE, OUT_SUMS, EXPERT_SUMS = (0, 1), (2, 3), (4, 5), (6, 7)
SUM_ORDER = EXPERT_SUMS + OUT_SUMS + EARLY + LATE
ROWS = (ROWS_A, ROWS_A, 2 * ROWS_W)


def unit_shape(unit):
    cores = (2,) if unit[0] < 2 else ()
    return cores + tuple(WIDE[axis] for axis in reversed(unit[3])) + (ROWS[unit[0]], unit[2])


def place():
    fsdp = lax.axis_index("fsdp")
    rep = lax.axis_index("rep")
    core = lax.rem(fsdp, 2)
    z = lax.rem(fsdp // 2, 4)
    y = lax.rem(fsdp // 8, 4)
    xl = fsdp // 32
    return {"x": xl, "y": y, "z": z, "c": core, "r": rep}


def device(at):
    return (at["x"] * 32 + at["y"] * 8 + at["z"] * 2 + at["c"], at["r"])


def shifted(at, axis, step):
    new = dict(at)
    if axis == "x":
        whole = lax.rem(at["r"] * 2 + at["x"] + step + 4, 4)
        new["x"] = lax.rem(whole, 2)
        new["r"] = whole // 2
    elif axis == "c":
        new["c"] = 1 - at["c"]
    else:
        new[axis] = lax.rem(at[axis] + step + 4, 4)
    return new


def greet(devices):
    barrier = pltpu.get_barrier_semaphore()
    for other in devices:
        pl.semaphore_signal(barrier, inc=1, device_id=device(other), device_id_type=MESH)


def meet(devices):
    pl.semaphore_wait(pltpu.get_barrier_semaphore(), len(devices))


ALL = slice(None)


class Piece:
    def __init__(self, order, spots, columns=ALL, rows=ALL):
        self.order, self.spots, self.columns, self.rows = order, spots, columns, rows

    def moved(self, axis, spot):
        return Piece(self.order, {**self.spots, axis: spot}, self.columns, self.rows)

    def full(self, axis):
        return self.moved(axis, (0, WIDE[axis]))

    def index(self, core, spots=None):
        spots = spots or self.spots
        lead = [spots[axis] for axis in reversed(self.order)]
        lead = [pl.ds(*spot) if isinstance(spot, tuple) else spot for spot in lead]
        return (*(() if core is None else (core,)), *lead, self.rows, self.columns)

    def of(self, ref, core):
        return ref.at[self.index(core)]

    def halves(self, rows, count):
        for axis in reversed(self.order):
            if isinstance(self.spots[axis], tuple):
                middle = WIDE[axis] // 2
                return [self.moved(axis, (0, middle)), self.moved(axis, (middle, middle))]
        first = count // 256 * 128
        return [Piece(self.order, self.spots, pl.ds(*run), ALL) for run in ((0, first), (first, count - first))]

    def shape(self, rows, count):
        lead = [self.spots[axis] for axis in reversed(self.order)]
        lead = tuple(spot[1] for spot in lead if isinstance(spot, tuple))
        size = [whole if part == ALL else part.size for part, whole in ((self.rows, rows), (self.columns, count))]
        return lead + tuple(size)


class Links:
    def __init__(self, at, send, recv, free, partners):
        self.at, self.send, self.recv, self.free, self.partners = at, send, recv, free, partners
        self.used, self.open = 0, []

    def turn(self):
        self.close()
        self.used, self.open = 0, []
        for other in self.partners:
            pl.semaphore_signal(self.free, inc=1, device_id=device(other), device_id_type=MESH)

    def turned(self):
        pl.semaphore_wait(self.free, len(self.partners))

    def local(self, source, target):
        copy = pltpu.make_async_copy(source, target, self.send.at[self.used])
        self.used += 1
        copy.start()
        return copy

    def push(self, source, target, to):
        copy = pltpu.make_async_remote_copy(
            src_ref=source,
            dst_ref=target,
            send_sem=self.send.at[self.used],
            recv_sem=self.recv.at[self.used],
            device_id=device(to),
            device_id_type=MESH,
        )
        self.used += 1
        copy.start()
        self.open.append(copy)
        return copy

    def close(self):
        for copy in self.open:
            copy.wait_send()


class Gather:
    def __init__(self, links, src, dst, unit):
        self.links, self.at, self.src, self.dst = links, links.at, src, dst
        array, self.first, self.count, self.order = unit
        self.rows = ROWS[array]
        self.core = self.at["c"] if array < 2 else None
        self.handed = []

    def push(self, source, piece, target):
        spot = piece.of(self.dst, self.core)
        return self.links.push(spot if source is None else source, spot, target)

    def sibling(self, piece, source=None):
        if self.core is None:
            return
        self.handed.append(self.push(source, piece, shifted(self.at, "c", 0)))

    def source_of(self, piece):
        columns = piece.columns
        if columns == ALL:
            columns = pl.ds(self.first, self.count)
        else:
            columns = pl.ds(self.first + columns.start, columns.size)
        return self.src.at[:, columns]

    def steps(self):
        at, order = self.at, self.order
        have = Piece(order, {axis: at[axis] for axis in order})
        if self.core is None:
            rows = pl.ds(pl.multiple_of(ROWS_W * at["c"], ROWS_W), ROWS_W)
            block = Piece(order, have.spots, ALL, rows)
            own, theirs = (src.at[:, pl.ds(self.first, self.count)] for src in self.src)
            local = self.links.local(own, block.of(self.dst, None))
            copy = self.push(theirs, block, shifted(at, "c", 0))
            yield
            local.wait()
            copy.wait_recv()
            mine = None
        else:
            mine = self.source_of(have)
            local = self.links.local(mine, have.of(self.dst, self.core))
        plane = order[: 2 if order[0] == "x" else 1] if self.core is not None else ""
        if plane:
            ring = plane[-1]
            direct = [self.push(mine, have, shifted(at, ring, step)) for step in (1, -1, 2)]
            if "x" in plane:
                halves = have.halves(self.rows, self.count)
                for step in (0, 1, -1, 2):
                    for half, side in zip(halves, (1, -1)):
                        target = shifted(shifted(at, "x", side), ring, step)
                        direct.append(self.push(self.source_of(half), half, target))
            yield
            local.wait()
            for copy in direct:
                copy.wait_recv()
        for axis in plane:
            have = have.full(axis)
        for axis in order[len(plane) :]:
            if axis == "x":
                halves = have.halves(self.rows, self.count)
                moved = [self.push(None, half, shifted(at, "x", side)) for half, side in zip(halves, (1, -1))]
                yield
                for copy in moved:
                    copy.wait_recv()
                self.sibling(have.moved("x", 1 - at["x"]))
                return
            near = [self.push(None, have, shifted(at, axis, step)) for step in (1, -1)]
            self.sibling(have)
            yield
            fresh = [have.moved(axis, shifted(at, axis, -step)[axis]) for step in (1, -1)]
            far = []
            for index, step in enumerate((1, -1)):
                near[index].wait_recv()
                piece = fresh[index].halves(self.rows, self.count)[index]
                far.append(self.push(None, piece, shifted(at, axis, step)))
            for piece in fresh:
                self.sibling(piece)
            yield
            for copy in far:
                copy.wait_recv()
            self.sibling(have.moved(axis, shifted(at, axis, 2)[axis]))
            have = have.full(axis)

    def settle(self):
        for copy in self.handed:
            copy.wait_recv()


class Group:
    def __init__(self, flows):
        self.flows = flows
        self.live = [flow.steps() for flow in flows]

    def step(self, times=1):
        for unused in range(times):
            self.live = [flow for flow in self.live if next(flow, "end") != "end"]

    def run(self):
        while self.live:
            self.step()

    def settle(self):
        self.run()
        for flow in self.flows:
            flow.settle()


def add_blocks(ref, piece, core, others):
    runs = [axis for axis in reversed(piece.order) if isinstance(piece.spots[axis], tuple)]
    loops = runs[:-1]
    total = 1
    for axis in loops:
        total *= piece.spots[axis][1]

    def step(i, carry):
        left, spots = i, dict(piece.spots)
        index = []
        for axis in reversed(loops):
            start, length = piece.spots[axis]
            spot = lax.rem(left, length)
            index.insert(0, spot)
            spots[axis] = start + spot
            left = left // length
        where = piece.index(core, spots)
        terms = [ref[where]]
        terms += [other[tuple(index) + (ALL,) * (len(other.shape) - len(index))] for other in others]
        if len(terms) > 2:
            terms = [term.astype(F32) for term in terms]
        ref[where] = functools.reduce(jnp.add, terms).astype(BF16)
        return carry

    if loops:
        lax.fori_loop(0, total, step, 0)
    else:
        step(0, 0)


class Scatter:
    def __init__(self, links, grad, out, unit, buffers):
        self.links, self.at, self.grad, self.out = links, links.at, grad, out
        array, self.first, self.count, self.order = unit
        self.unit, self.rows = unit, ROWS[array]
        self.buffers = list(buffers)

    @staticmethod
    def shapes(unit):
        rows, count, order = ROWS[unit[0]], unit[2], unit[3]
        piece = Piece(order, {axis: (0, WIDE[axis]) for axis in order})
        shapes = [piece.shape(rows, count)] if unit[0] < 2 else []
        rest = list(reversed(order))
        if order[-1] == "x":
            piece = piece.moved("x", 0)
            shapes += [half.shape(rows, count) for half in piece.halves(rows, count)]
            rest.pop(0)
        piece = piece.moved(rest[0], 0)
        shapes += [half.shape(rows, count) for half in piece.halves(rows, count)]
        shapes += [piece.shape(rows, count)] * 2
        piece = piece.moved(rest[1], 0)
        if unit[0] < 2:
            shapes += [piece.shape(rows, count)] * 3
        else:
            shapes += [half.shape(rows, count) for half in piece.halves(rows, count)]
            shapes += [piece.shape(rows, count)] * 2
        return shapes + [(rows, count)] * (3 if order[0] == "x" else 1)

    def push(self, piece, core, target):
        buffer = self.buffers.pop(0)
        return self.links.push(piece.of(self.grad, core), buffer, target), buffer

    def steps(self):
        at, rows, count = self.at, self.rows, self.count
        core = at["c"] if self.unit[0] < 2 else None
        piece = Piece(self.order, {axis: (0, WIDE[axis]) for axis in self.order})
        last = self.order[-1]
        if core is not None:
            copy, buffer = self.push(piece, 1 - core, shifted(at, "c", 0))
            yield
            copy.wait_recv()
            add_blocks(self.grad, piece, core, [buffer])
        rest = list(reversed(self.order))
        if last == "x":
            theirs = piece.moved("x", 1 - at["x"]).halves(rows, count)
            moved = [self.push(half, core, shifted(at, "x", step)) for half, step in zip(theirs, (1, -1))]
            yield
            piece = piece.moved("x", at["x"])
            for (copy, buffer), half in zip(moved, piece.halves(rows, count)):
                copy.wait_recv()
                add_blocks(self.grad, half, core, [buffer])
            rest.pop(0)
        for axis in rest[: 1 if core is not None else 2]:
            theirs = piece.moved(axis, shifted(at, axis, 2)[axis]).halves(rows, count)
            far = [self.push(half, core, shifted(at, axis, step)) for half, step in zip(theirs, (1, -1))]
            yield
            near = []
            for index, step in enumerate((1, -1)):
                theirs = piece.moved(axis, shifted(at, axis, step)[axis])
                copy, buffer = far[index]
                copy.wait_recv()
                add_blocks(self.grad, theirs.halves(rows, count)[index], core, [buffer])
                near.append(self.push(theirs, core, shifted(at, axis, step)))
            yield
            piece = piece.moved(axis, at[axis])
            for copy, buffer in near:
                copy.wait_recv()
            add_blocks(self.grad, piece, core, [buffer for copy, buffer in near])
        if core is not None:
            ring = rest[1]
            moves = [shifted(at, ring, step) for step in (1, -1, 2)]
            direct = [self.push(piece.moved(ring, to[ring]), core, to) for to in moves]
            yield
            piece = piece.moved(ring, at[ring])
            for copy, buffer in direct:
                copy.wait_recv()
            add_blocks(self.grad, piece, core, [buffer for copy, buffer in direct])
        if self.order[0] == "x":
            other = piece.moved("x", 1 - at["x"])
            piece = piece.moved("x", at["x"])
            ends = [self.push(piece, core, shifted(at, "x", 2))]
            ends += [self.push(other, core, shifted(at, "x", side)) for side in (1, -1)]
        else:
            ends = [self.push(piece, core, shifted(at, "x", 2))]
        yield
        for copy, buffer in ends:
            copy.wait_recv()
        total = self.grad[piece.index(core)].astype(F32) + ends[0][1][...].astype(F32)
        if len(ends) > 1:
            total = total + (ends[1][1][...].astype(F32) + ends[2][1][...].astype(F32))
        if core is not None:
            self.out[:, pl.ds(self.first, count)] = total
            return
        sums, shared, arriving = self.out
        lower = pl.multiple_of(ROWS_W * at["c"], ROWS_W)
        columns = pl.ds(self.first, count)
        shared[:, columns] = total
        theirs = shared.at[pl.ds(ROWS_W - lower, ROWS_W), columns]
        copy = self.links.push(theirs, arriving.at[:, columns], shifted(at, "c", 0))
        yield
        copy.wait_recv()
        for tile in range(self.first // 128, (self.first + count) // 128):
            local = pl.ds(128 * tile, 128)
            base = FF * (tile // 2) + 128 * (tile % 2)
            mine = pl.ds(pl.multiple_of(base + 256 * at["c"], 128), 128)
            other = pl.ds(pl.multiple_of(base + 256 * (1 - at["c"]), 128), 128)
            sums[:, mine] = shared[pl.ds(lower, ROWS_W), local]
            sums[:, other] = arriving[:, local]

    def settle(self):
        pass


def mm(a, b):
    return jnp.dot(a, b, preferred_element_type=F32)


def mm_nt(a, b):
    return lax.dot_general(a, b, (((1,), (1,)), ((), ())), preferred_element_type=F32)


def mm_tn(a, b):
    return lax.dot_general(a, b, (((0,), (0,)), ((), ())), preferred_element_type=F32)


def turn(value, cosine, sine):
    width = value.shape[1]
    lane = lax.broadcasted_iota(jnp.int32, (1, width), 1)
    low = lax.rem(lane, 64) < 32
    swapped = jnp.where(low, pltpu.roll(value, width - 32, 1), pltpu.roll(value, 32, 1))
    return value * cosine + swapped * sine


def doubled(block, odd, low):
    other = pltpu.roll(block.astype(F32), 64, 1).astype(BF16)
    return jnp.where(low, other, block) if odd else jnp.where(low, block, other)


def split_two(value):
    top = value.astype(BF16)
    return top, (value - top.astype(F32)).astype(BF16)


LAYER_SCRATCH = (
    pltpu.VMEM((ROWS_A, MISC + 128), BF16),
    pltpu.VMEM((ROWS_A, MISC), F32),
    pltpu.VMEM((ROWS_A, D + 128), F32),
    pltpu.VMEM((ROWS_W, SHARE), BF16),
    pltpu.VMEM((ROWS_W, SHARE), BF16),
    pltpu.VMEM((2 * ROWS_W, SHARE), F32),
    pltpu.VMEM((ROWS_W, SHARE), F32),
    pltpu.VMEM((TOK, 2048), BF16),
    pltpu.VMEM((TOK, D), BF16),
    pltpu.VMEM((8, 2 * TOK, TOK), F32),
    pltpu.VMEM((TOK, 2048), BF16),
    pltpu.VMEM((TOK, D), BF16),
    pltpu.VMEM((TOK, D), BF16),
    pltpu.VMEM((TOK, D), F32),
    pltpu.VMEM((TOK, D), F32),
    pltpu.VMEM((TOK, D), F32),
    pltpu.VMEM((D, TOK), BF16),
    pltpu.VMEM((D, TOK), BF16),
    pltpu.VMEM((4 * TOK, EXTRA), BF16),
    pltpu.VMEM((4 * TOK, D), BF16),
    pltpu.VMEM((2, 4 * TOK, SHARE), BF16),
    pltpu.VMEM((2 * TOK, D), F32),
    pltpu.VMEM((2 * TOK, D), F32),
    pltpu.VMEM((4 * TOK, 128), F32),
    pltpu.VMEM((2 * TOK, EXTRA), BF16),
    pltpu.VMEM((2 * TOK, EXTRA), BF16),
    pltpu.VMEM((TOK, EXTRA), BF16),
    pltpu.VMEM((TOK, EXTRA), BF16),
    pltpu.VMEM((2 * TOK, D), BF16),
    pltpu.VMEM((2 * TOK, D), BF16),
    pltpu.VMEM((TOK, D), BF16),
    pltpu.VMEM((TOK, D), BF16),
    pltpu.VMEM((D, 4 * TOK), BF16),
    pltpu.VMEM((D, 4 * TOK), BF16),
)


def whole_body(
    x_ref, g_ref, seg_ref, route_ref, in_ref, aout_ref, gain1_ref, gain2_ref, router_ref, expert_ref,
    out_ref, dx_ref, sum_in, sum_out, small_ref, sum_w,
    src_in, sum_all, sum_more, src_own, src_peer, shared, arriving, qkv, attn, probs, dqkv, a1_ref, dattn_ref, h_ref, dh_ref, da1_ref, a1t, attnt,
    a2_all, g_all, mid, da2_ref, y_ref, dg_ref, sib_d, from_d, ret_d, got_d, sib_y, from_y, ret_y, got_y, a2t, gt, *rest,
):
    at = place()
    ahead, behind = shifted(at, "x", 1), shifted(at, "x", -1)

    around = [shifted(at, axis, step) for axis in "yz" for step in (1, -1, 2)]
    around += [shifted(shifted(at, "x", side), axis, step) for axis in "yz" for step in (1, -1, 2) for side in (1, -1)]
    around += [shifted(at, "x", step) for step in (1, -1, 2)]
    around += [shifted(at, "c", 0)]
    links = Links(at, *rest[-5:-2], around)
    pairs = Links(at, *rest[-2:], None, None)
    greet(around)

    eight = lax.broadcasted_iota(jnp.int32, (8, 128), 0)
    eye = jnp.where(eight == lax.broadcasted_iota(jnp.int32, (8, 128), 1), 1.0, 0.0)
    small = [ref[...].astype(F32) for ref in (router_ref, gain1_ref, gain2_ref)]
    small = jnp.concatenate(small + [jnp.zeros((2, ROWS_A), F32)], axis=0)
    src_in[:, pl.ds(MISC, 128)] = mm_tn(small.astype(BF16), eye.astype(BF16)).astype(BF16)
    for slot, tile in enumerate(TILES):
        src_in[:, pl.ds(256 * slot, 256)] = in_ref[:, pl.ds(256 * tile, 256)]

    for index in range(3):
        target = pl.ds(256 * index, 256)
        for half, columns in ((at["c"], src_own), (1 - at["c"], src_peer)):
            columns[:, target] = expert_ref[:, pl.ds(pl.multiple_of(FF * index + 256 * half, 256), 256)]

    meet(around)

    sources = (src_in, aout_ref, (src_own, src_peer))
    sums = (sum_all, sum_more, (sum_w, shared, arriving))
    buffers = list(rest[:-5])

    weights, grads = buffers[: len(GATHERS)], buffers[len(GATHERS) : len(GATHERS) + len(SUMS)]
    del buffers[: len(GATHERS) + len(SUMS)]

    def gathers(units):
        return Group([Gather(links, sources[GATHERS[u][0]], weights[u], GATHERS[u]) for u in units])

    def scatters(*units):
        flows = []
        for u in units:
            number = len(Scatter.shapes(SUMS[u]))
            mine = buffers[:number]
            del buffers[:number]
            flows.append(Scatter(links, grads[u], sums[SUMS[u][0]], SUMS[u], mine))
        return Group(flows)

    def swap(source, target, first_source, first_target):
        rows = ((0, ahead), (HALF, behind))
        return [
            pairs.push(
                source.at[pl.ds(first_source + lower, HALF)], target.at[pl.ds(first_target + lower, HALF)], to
            )
            for lower, to in rows
        ]

    def swap_back(source, target):
        rows = ((0, behind), (HALF, ahead))
        return [
            pairs.push(source.at[pl.ds(lower, HALF)], target.at[pl.ds(lower, HALF)], to) for lower, to in rows
        ]

    def arrived(copies):
        for copy in copies:
            copy.wait_recv()

    def spot(unit, **where):
        return tuple(where[axis] for axis in ("c",) + tuple(reversed(unit[3])))

    def blocks_a(xs=(0, 1), ys=(0, 1, 2, 3)):
        return [dict(x=x, y=y, z=z, c=c) for x in xs for y in ys for z in range(4) for c in range(2)]

    def cols_a(u, lower, count, **some):
        return jnp.concatenate(
            [weights[u][spot(GATHERS[u], **where) + (ALL, pl.ds(lower, count))] for where in blocks_a(**some)],
            axis=0,
        )

    def tile_a(u, t, count, lower=0):
        return cols_a(u, lower, count, xs=(t // 2,), ys=(2 * (t % 2), 2 * (t % 2) + 1))

    def put_a(u, lower, value):
        value, count = value.astype(BF16), value.shape[1]
        for i, where in enumerate(blocks_a()):
            grads[u][spot(SUMS[u], **where) + (ALL, pl.ds(lower, count))] = value[ROWS_A * i : ROWS_A * (i + 1)]

    def blocks_w(el, ys=(0, 1), zs=(0, 1, 2, 3)):
        return [dict(y=2 * el + y, z=z) for y in ys for z in zs]

    def spot_w(unit, y, z):
        return (z, y) if unit[3] == "yz" else (y, z)

    def cols_w(el, lower, count, **some):
        runs = []
        for u, start in zip(EXPERTS_IN, (0, 384)):
            low_col, high_col = max(lower, start), min(lower + count, start + 384)
            if low_col < high_col:
                columns = pl.ds(low_col - start, high_col - low_col)
                blocks = [weights[u][spot_w(GATHERS[u], **at_w) + (ALL, columns)] for at_w in blocks_w(el, **some)]
                runs.append(jnp.concatenate(blocks, axis=0))
        return runs[0] if len(runs) == 1 else jnp.concatenate(runs, axis=1)

    def put_w(el, lower, value):
        value, count = value.astype(BF16), value.shape[1]
        for u, start in zip(EXPERT_SUMS, (0, 384)):
            low_col, high_col = max(lower, start), min(lower + count, start + 384)
            if low_col < high_col:
                columns = pl.ds(low_col - start, high_col - low_col)
                for i, at_w in enumerate(blocks_w(el)):
                    block = value[128 * i : 128 * (i + 1), low_col - lower : high_col - lower]
                    grads[u][spot_w(SUMS[u], **at_w) + (ALL, columns)] = block

    inputs, outputs, experts = gathers(INPUTS), gathers(OUTPUTS), gathers(EXPERTS_IN)
    inputs.step()
    experts.step()

    own = pl.ds(0, TOK)
    g_all[own, :] = g_ref[...]
    x = x_ref[...].astype(F32)
    r1 = lax.rsqrt(jnp.mean(x * x, axis=1, keepdims=True) + EPS)
    ids = jnp.concatenate([seg_ref[0:1, :], seg_ref[1:2, :] + 4], axis=1).astype(F32)
    rows = jnp.concatenate([ids, route_ref[...].astype(F32), jnp.zeros((TOK - 3, TOK), F32)], axis=0)
    columns = rows.T
    lane = lax.broadcasted_iota(jnp.int32, (1, 128), 1)
    low = lane < 64
    same = columns[:, 0:1] == ids
    t_index = lax.broadcasted_iota(jnp.int32, (TOK, TOK), 0)
    u_index = lax.broadcasted_iota(jnp.int32, (TOK, TOK), 1)
    pos = jnp.sum(jnp.where(same & (u_index < t_index), 1.0, 0.0), axis=1, keepdims=True)
    allowed = same & (u_index <= t_index)
    allowed2 = jnp.concatenate([allowed, allowed], axis=0)
    route0, route1 = columns[:, 1:2].astype(jnp.int32), columns[:, 2:3].astype(jnp.int32)
    named = (route0 == lane) | (route1 == lane)
    inputs.step()
    outputs.step()
    experts.step()
    power = lax.rem(lane, 32).astype(F32) * (2.0 / 64)
    angle = pos * jnp.exp(power * (-9.210340371976184))
    cosine = jnp.cos(angle)
    sine = jnp.where(lax.rem(lane, 64) < 32, -1.0, 1.0) * jnp.sin(angle)
    cos4 = jnp.concatenate([cosine] * 2, axis=1)
    sin4 = jnp.concatenate([sine] * 2, axis=1)
    inputs.step()
    outputs.step()
    experts.step()
    inputs.run()
    outputs.step()
    experts.step()
    inputs.settle()

    misc = cols_a(1, 1024, 128)
    row = lax.broadcasted_iota(jnp.int32, (16, 128), 0)
    lane16 = lax.broadcasted_iota(jnp.int32, (16, 128), 1)
    gains = mm_nt(jnp.where(lane16 == row + 4, 1.0, 0.0).astype(BF16), misc)
    gain1, gain2 = gains[0:1], gains[1:2]
    a1_ref[...] = (x * r1 * gain1).astype(BF16)
    for j in range(8):
        block = mm(a1_ref[...], cols_a(j // 4, 256 * (j % 4), 256))
        if TILES[j] < 6:
            block = turn(block, cos4, sin4)
        qkv[:, pl.ds(256 * TILES[j], 256)] = block.astype(BF16)
        if j == 0:
            g_copies = swap(g_ref, g_all, 0, TOK)
            g_own = pairs.push(g_ref, g_all.at[pl.ds(2 * TOK, TOK)], shifted(at, "c", 0))
    outputs.step()

    def heads(ref, k):
        pair = ref[:, pl.ds(128 * k, 128)]
        zero = jnp.zeros_like(pair)
        return jnp.concatenate([jnp.where(low, pair, zero), jnp.where(low, zero, pair)], axis=0)

    def keys(k):
        return doubled(qkv[:, pl.ds(1024 + 128 * (k // 2), 128)], k % 2, low)

    def values(k):
        return doubled(qkv[:, pl.ds(1536 + 128 * (k // 2), 128)], k % 2, low)

    for first in (0, 4):
        some = range(first, first + 4)
        scores = [mm_nt(heads(qkv, k), keys(k)) * 0.125 for k in some]
        scores = [jnp.where(allowed2, score, -1000000000.0) for score in scores]
        peaks = [jnp.max(score, axis=1, keepdims=True) for score in scores]
        raised = [jnp.exp(score - peak) for score, peak in zip(scores, peaks)]
        scales = [1.0 / jnp.sum(value, axis=1, keepdims=True) for value in raised]
        prob = [value * scale for value, scale in zip(raised, scales)]
        both = [mm(value.astype(BF16), values(k)) for value, k in zip(prob, some)]
        for k, value, pair in zip(some, prob, both):
            probs[k] = value
            attn[:, pl.ds(128 * k, 128)] = jnp.where(low, pair[:TOK], pair[TOK:]).astype(BF16)
        if first == 0:
            outputs.run()
        else:
            experts.step()
    a1t[...] = a1_ref[...].T
    outputs.settle()

    for j in range(4):
        part_j = pl.ds(256 * j, 256)
        h_ref[:, part_j] = x_ref[:, part_j].astype(F32) + mm(
            attn[...], cols_a(OUTPUTS[j // 2], 256 * (j % 2), 256)
        )
    h = h_ref[...]
    r2 = lax.rsqrt(jnp.mean(h * h, axis=1, keepdims=True) + EPS)
    a2 = (h * r2 * gain2).astype(BF16)
    a2_all[own, pl.ds(0, D)] = a2
    logits = jnp.where(lane < EXPERTS, mm(a2, misc), -jnp.inf)
    lexp = jnp.exp(logits - jnp.max(logits, axis=1, keepdims=True))
    rprobs = lexp / jnp.sum(lexp, axis=1, keepdims=True)
    gates = jnp.where(named, rprobs, 0.0)
    top, rest_of = split_two(gates)
    a2_all[own, pl.ds(D, 128)] = (top.astype(F32) + pltpu.roll(rest_of.astype(F32), EXPERTS, 1)).astype(BF16)
    a2_copies = swap(a2_all, a2_all, 0, TOK)
    experts.run()
    sibling = shifted(at, "c", 0)
    beside, across = pl.ds(TOK, TOK), pl.ds(3 * TOK, TOK)
    a2_own = pairs.push(a2_all.at[own], a2_all.at[pl.ds(2 * TOK, TOK)], sibling)
    arrived(g_copies)
    g_on = pairs.push(g_all.at[beside], g_all.at[across], sibling)
    arrived([g_own, g_on])
    gt[...] = g_all[...].T
    attnt[...] = attn[...].T
    experts.settle()
    links.turn()
    arrived(a2_copies)
    a2_on = pairs.push(a2_all.at[beside], a2_all.at[across], sibling)
    arrived([a2_own, a2_on])

    dgates = jnp.zeros((4 * TOK, 128), F32)
    for el in range(2):
        e = 2 * at["x"] + el
        extra = a2_all[:, pl.ds(D, 128)].astype(F32)
        gate_e = jnp.sum(jnp.where((lane == e) | (lane == e + EXPERTS), extra, 0.0), axis=1, keepdims=True)
        v = mm(a2_all[:, pl.ds(0, D)], cols_w(el, 0, 256))
        up = mm(a2_all[:, pl.ds(0, D)], cols_w(el, 256, 256))
        back = mm(g_all[...], cols_w(el, 512, 256))
        s = 1.0 / (1.0 + jnp.exp(-v))
        silu = v * s
        hidden = (silu * up).astype(BF16).astype(F32)
        dgates = dgates + jnp.where(lane == e, jnp.sum(hidden * back, axis=1, keepdims=True), 0.0)
        back = back * gate_e
        mid[el, :, pl.ds(0, 256)] = (back * up * s * (1.0 + v * (1.0 - s))).astype(BF16)
        mid[el, :, pl.ds(256, 256)] = (back * silu).astype(BF16)
        mid[el, :, pl.ds(512, 256)] = (hidden * gate_e).astype(BF16)
    dg_ref[...] = dgates

    def tile_w(el, t, lower, count):
        return cols_w(el, lower, count, ys=(t // 2,), zs=(2 * lax.rem(t, 2), 2 * lax.rem(t, 2) + 1))

    def da2_tile(t, carry):
        total = jnp.zeros((4 * TOK, 256), F32)
        for el in range(2):
            total = total + mm_nt(mid[el, :, pl.ds(0, 512)], tile_w(el, t, 0, 512))
        columns = pl.ds(pl.multiple_of(256 * t, 256), 256)
        da2_ref[:, columns] = total[: 2 * TOK]
        sib_d[:, columns] = total[2 * TOK :].astype(BF16)
        return carry

    def two_lanes(value):
        top, rest_of = split_two(value)
        return (top.astype(F32) + pltpu.roll(rest_of.astype(F32), EXPERTS, 1)).astype(BF16)

    def one_lane(extra):
        extra = extra.astype(F32)
        return extra + pltpu.roll(extra, 128 - EXPERTS, 1)

    lax.fori_loop(0, 4, da2_tile, 0)
    gates_at = pl.ds(D, 128)
    sib_d[:, gates_at] = two_lanes(dg_ref[pl.ds(2 * TOK, 2 * TOK), :])
    sib_copy = pairs.push(sib_d, from_d, sibling)
    a2t[...] = a2_all[:, pl.ds(0, D)].T
    sib_copy.wait_recv()
    ret_d[:, pl.ds(0, D)] = (da2_ref[beside, :] + from_d[beside, pl.ds(0, D)].astype(F32)).astype(BF16)
    ret_d[:, gates_at] = two_lanes(
        jnp.where(lane < EXPERTS, dg_ref[beside, :] + one_lane(from_d[beside, gates_at]), 0.0)
    )
    d_copies = swap_back(ret_d, got_d)

    for el in range(2):
        for j in range(3):
            left = a2t if j < 2 else gt
            put_w(el, 256 * j, mm(left[...], mid[el, :, pl.ds(256 * j, 256)]))
    links.turned()
    expert_sums = scatters(*EXPERT_SUMS)
    expert_sums.step()

    def y_tile(t, carry):
        total = jnp.zeros((4 * TOK, 256), F32)
        for el in range(2):
            total = total + mm_nt(mid[el, :, pl.ds(512, 256)], tile_w(el, t, 512, 256))
        columns = pl.ds(pl.multiple_of(256 * t, 256), 256)
        y_ref[:, columns] = total[: 2 * TOK]
        sib_y[:, columns] = total[2 * TOK :].astype(BF16)
        return carry

    lax.fori_loop(0, 4, y_tile, 0)
    y_own = pairs.push(sib_y, from_y, sibling)

    arrived(d_copies)
    dgates = dg_ref[own, :] + one_lane(from_d[own, gates_at]) + one_lane(got_d[:, gates_at])
    dp = jnp.where(named, dgates, 0.0)
    dlogits = (rprobs * (dp - jnp.sum(rprobs * dp, axis=1, keepdims=True))).astype(BF16)
    da2 = da2_ref[own, :] + from_d[own, pl.ds(0, D)].astype(F32) + got_d[:, pl.ds(0, D)].astype(F32)
    da2 = da2 + mm_nt(dlogits, misc)
    h = h_ref[...]
    misc_grad = mm_tn(a2_all[own, pl.ds(0, D)], dlogits)
    gain_two = (da2 * h * r2).astype(BF16)
    scaled = gain2 * da2
    dh = g_ref[...].astype(F32) + r2 * scaled - h * (r2 * r2 * r2) * jnp.mean(scaled * h, axis=1, keepdims=True)
    branch = dh.astype(BF16)
    dh_ref[...] = dh
    for j in range(4):
        put_a(OUT_SUMS[j // 2], 256 * (j % 2), mm(attnt[...], branch[:, 256 * j : 256 * j + 256]))
    misc_grad = misc_grad + mm_tn(gain_two, jnp.where(u_index == 5, 1.0, 0.0).astype(BF16))
    put_a(OUT_SUMS[1], 512, misc_grad)
    out_sums = scatters(*OUT_SUMS)
    out_sums.step()
    for t in range(4):
        dattn = mm_nt(branch[:, :512], tile_a(OUTPUTS[0], t, 512)) + mm_nt(branch[:, 512:], tile_a(OUTPUTS[1], t, 512))
        dattn_ref[:, pl.ds(256 * t, 256)] = dattn.astype(BF16)

    y_own.wait_recv()
    ret_y[...] = (y_ref[beside, :] + from_y[beside, :].astype(F32)).astype(BF16)
    y_copies = swap_back(ret_y, got_y)
    for first in (0, 4):
        some = range(first, first + 4)
        stacks = [heads(dattn_ref, k) for k in some]
        dprob = [mm_nt(stack, values(k)) for stack, k in zip(stacks, some)]
        parts = [probs[k] * value for k, value in zip(some, dprob)]
        sums_of = [jnp.sum(value, axis=1, keepdims=True) for value in parts]
        ds = [(value - probs[k] * total).astype(BF16) for k, value, total in zip(some, parts, sums_of)]
        dq = [mm(value, keys(k)) * 0.125 for value, k in zip(ds, some)]
        dk = [mm_tn(value, heads(qkv, k)) * 0.125 for value, k in zip(ds, some)]
        dv = [mm_tn(probs[k].astype(BF16), stack) for k, stack in zip(some, stacks)]
        dk = [value + pltpu.roll(value, 64, 1) for value in dk]
        dv = [value + pltpu.roll(value, 64, 1) for value in dv]
        for k, value in zip(some, dq):
            value = jnp.where(low, value[:TOK], value[TOK:])
            dqkv[:, pl.ds(128 * k, 128)] = turn(value, cosine, -sine).astype(BF16)
        for i in (0, 2):
            column = 64 * (first + i)
            value = turn(jnp.where(low, dk[i], dk[i + 1]), cosine, -sine)
            dqkv[:, pl.ds(1024 + column, 128)] = value.astype(BF16)
            dqkv[:, pl.ds(1536 + column, 128)] = jnp.where(low, dv[i], dv[i + 1]).astype(BF16)
        if first == 0:
            early = scatters(*EARLY)
            for j in range(4):
                put_a(j // 2, 256 * (j % 2), mm(a1t[...], dqkv[:, pl.ds(256 * TILES[j], 256)]))
            early.step()
            expert_sums.step()
            out_sums.step()
    late = [scatters(u) for u in LATE]
    for j in range(4, 8):
        put_a(j // 2, 256 * (j % 2), mm(a1t[...], dqkv[:, pl.ds(256 * TILES[j], 256)]))
        if j % 2:
            late[j // 2 - 2].step()
    early.step()
    out_sums.step()
    expert_sums.step()
    for t in range(4):
        total = jnp.zeros((TOK, 256), F32)
        for j in range(8):
            left = dqkv[:, pl.ds(256 * TILES[j], 256)]
            total = total + mm_nt(left, tile_a(j // 4, t, 256, 256 * (j % 4)))
        da1_ref[:, pl.ds(256 * t, 256)] = total
    da1 = da1_ref[...]
    x = x_ref[...].astype(F32)
    for group in late:
        group.step()
    scaled = gain1 * da1
    dx_ref[...] = (
        dh_ref[...] + r1 * scaled - x * (r1 * r1 * r1) * jnp.mean(scaled * x, axis=1, keepdims=True)
    )
    for group in late:
        group.step()
    early.step()
    out_sums.step()
    expert_sums.step()
    arrived(y_copies)
    out_ref[...] = (
        h_ref[...] + y_ref[own, :] + from_y[own, :].astype(F32) + got_y[...].astype(F32)
    ).astype(BF16)
    groups = late + [early, out_sums, expert_sums]
    while any(group.live for group in groups):
        for group in groups:
            group.step()
    product = jnp.zeros((ROWS_A, 1), F32)
    for slot, tile in enumerate(TILES):
        block = sum_all[:, pl.ds(256 * slot, 256)]
        sum_in[:, pl.ds(256 * tile, 256)] = block
        product = product + jnp.sum(block * in_ref[:, pl.ds(256 * tile, 256)].astype(F32), axis=1, keepdims=True)
    sum_out[...] = sum_more[:, pl.ds(0, D)]
    own_gain = jnp.sum(jnp.where(lane == 4, src_in[:, pl.ds(MISC, 128)].astype(F32), 0.0), axis=1, keepdims=True)
    tail = jnp.where(lane == 4, product / own_gain, sum_more[:, pl.ds(D, 128)])
    tail = jnp.concatenate([tail, jnp.zeros((128 - ROWS_A, 128), F32)], axis=0)
    small_ref[...] = tail.T[:8, :ROWS_A]
    links.close()
    pairs.close()


SEMS = 92
PAIR_SEMS = 14
VMEM_LIMIT = 60 * 1024 * 1024


def whole(tokens, cotangent, seg, routes, attn_in, attn_out, gain_attn, gain_ffn, router, expert_weight):
    buffers = [pltpu.VMEM(unit_shape(unit), BF16) for unit in GATHERS + SUMS]
    buffers += [pltpu.VMEM(shape, BF16) for u in SUM_ORDER for shape in Scatter.shapes(SUMS[u])]
    vmem = pl.BlockSpec(memory_space=pltpu.VMEM)
    return pl.pallas_call(
        whole_body,
        out_shape=(
            jax.ShapeDtypeStruct((TOK, D), BF16),
            jax.ShapeDtypeStruct((TOK, D), F32),
            jax.ShapeDtypeStruct((ROWS_A, 2048), F32),
            jax.ShapeDtypeStruct((ROWS_A, D), F32),
            jax.ShapeDtypeStruct((8, ROWS_A), F32),
            jax.ShapeDtypeStruct((ROWS_W, COLS_W), F32),
        ),
        in_specs=[vmem] * 10,
        out_specs=(vmem,) * 6,
        scratch_shapes=list(LAYER_SCRATCH)
        + buffers
        + [pltpu.SemaphoreType.DMA((SEMS,)), pltpu.SemaphoreType.DMA((SEMS,)), pltpu.SemaphoreType.REGULAR]
        + [pltpu.SemaphoreType.DMA((PAIR_SEMS,))] * 2,
        compiler_params=pltpu.CompilerParams(
            collective_id=0, has_side_effects=True, vmem_limit_bytes=VMEM_LIMIT
        ),
    )(tokens, cotangent, seg, routes, attn_in, attn_out, gain_attn, gain_ffn, router, expert_weight)


def emit_body(*refs):
    big, small, outs = refs[:5], refs[5], refs[6:]
    for source, target in zip(big, outs):
        target[...] = source[...]
    router, gain1, gain2 = outs[5:]
    router[...] = small[0:4, :]
    gain1[...] = small[4:5, :]
    gain2[...] = small[5:6, :]


def emit(big, small):
    vmem = pl.BlockSpec(memory_space=pltpu.VMEM)
    shapes = [jax.ShapeDtypeStruct(value.shape, value.dtype) for value in big]
    shapes += [jax.ShapeDtypeStruct((rows, ROWS_A), F32) for rows in (EXPERTS, 1, 1)]
    return pl.pallas_call(
        emit_body, out_shape=tuple(shapes), in_specs=[vmem] * 6, out_specs=(vmem,) * 8
    )(*big, small)


def local(
    tokens, segment_ids, routes, gain_attn, attn_in, attn_out, gain_ffn, router, expert_weight, cotangent
):
    output, grad, sum_in, sum_out, small, sum_w = whole(
        tokens, cotangent, segment_ids, routes.T, attn_in, attn_out,
        gain_attn[None, :], gain_ffn[None, :], router.T, expert_weight,
    )
    output, grad, sum_in, sum_out, sum_w, router_grad, gain1, gain2 = emit(
        (output, grad, sum_in, sum_out, sum_w), small
    )
    return (output, grad, gain1[0], sum_in, sum_out, gain2[0], router_grad.T, sum_w)


def solution(mesh):
    return jax.shard_map(
        local,
        mesh=mesh,
        in_specs=(
            P(("fsdp", "rep"), None),
            P(("fsdp", "rep"), None),
            P(("fsdp", "rep"), None),
            P("fsdp"),
            P("fsdp", None),
            P("fsdp", None),
            P("fsdp"),
            P("fsdp", None),
            P("fsdp", None),
            P(("fsdp", "rep"), None),
        ),
        out_specs=(
            P(("fsdp", "rep"), None),
            P(("fsdp", "rep"), None),
            P("fsdp"),
            P("fsdp", None),
            P("fsdp", None),
            P("fsdp"),
            P("fsdp", None),
            P("fsdp", None),
        ),
        check_vma=False,
    )
```
